256 devices in a mesh: rows: 8 (over y, x_hi), blk: 16 (over z, x_lo), rep: 2 (over core).
Axes of the slice: x: 4 (x_hi: 2, x_lo: 2; x = x_hi * 2 + x_lo), y: 4, z: 8, core: 2. Of those that a mesh axis runs over, the one named last changes fastest.
Arguments:
- pair_left: bfloat16 [1024, 256, 128], P(('rep', 'rows'), 'blk'), parts along dimension 0, may hold values from -6 to 6
- pair_right: bfloat16 [1024, 256, 128], P(('rep', 'blk'), 'rows'), parts along dimension 0, may hold values from -6 to 6
- pair_middle: bfloat16 [1024, 512, 128], P(('rep', 'rows'), 'blk'), parts along dimension 0, may hold values from -6 to 6
- cotangent: bfloat16 [1024, 512, 128], P(('rep', 'rows'), 'blk'), parts along dimension 0, may hold values from -6 to 6
- left_weight: bfloat16 [128, 256], replicated, may hold values from -0.5 to 0.5
- right_weight: bfloat16 [128, 256], replicated, may hold values from -0.5 to 0.5
- gate_weight: bfloat16 [128, 128], replicated, may hold values from -0.5 to 0.5
- output_weight: bfloat16 [128, 128], replicated, may hold values from -0.5 to 0.5
Outputs:
- update: bfloat16 [1024, 512, 128], P(('rep', 'rows'), 'blk'), parts along dimension 0
- grad_left: bfloat16 [1024, 256, 128], P(('rep', 'rows'), 'blk'), parts along dimension 0
- grad_right: bfloat16 [1024, 256, 128], P(('rep', 'blk'), 'rows'), parts along dimension 0
- grad_middle: bfloat16 [1024, 512, 128], P(('rep', 'rows'), 'blk'), parts along dimension 0
- left_delta: float32 [256, 256], P('rep'), parts along dimension 0
- right_delta: float32 [256, 256], P('rep'), parts along dimension 0
- gate_delta: float32 [256, 128], P('rep'), parts along dimension 0
- output_delta: float32 [256, 128], P('rep'), parts along dimension 0
The draws below stay inside these ranges and needn't reach their ends.
There are 2 independent parts, one for each index of `rep`. The reference program is written for one: setup_inputs(seed, part) draws one part's arguments, and reference() takes and returns one part's arrays. A program takes and returns all parts, laid end to end along the dimension named above; an argument that names none is the same for every part. Nothing has to cross between parts.
All inputs are finite; a program needn't handle non-finite values.
Results may differ from the reference program's by a relative error of at most 0.025.
Values may be sent and summed in bfloat16 or wider, within the bound.
A program may use at most 64 MiB of HBM per device.

```python
import jax
import jax.numpy as jnp
from jax import lax

C = 128
CH = 128
ID = 64
JD = 32
I = 512
J = 512
K = 256
N_ROWS = 8
N_BLK = 16


def levels(rng, extent, cuts, low, top_value):
    def one(axis_at, blocks):
        draws = jax.random.uniform(jax.random.fold_in(jax.random.fold_in(rng, 6), axis_at), (blocks,), jnp.float32, low / len(cuts), top_value / len(cuts))
        return jnp.repeat(jnp.exp(draws), extent[axis_at] // blocks).reshape((-1,) + (1,) * (len(extent) - axis_at - 1))

    level = one(*cuts[0])
    for cut in cuts[1:]:
        level = level * one(*cut)
    return level


def normal_values(key, extent, spread, limit, pieces=(), kind=jnp.bfloat16):
    values = spread * jax.random.normal(key, extent, jnp.float32)
    if pieces:
        values = values * levels(key, extent, pieces, -0.22, 0.18)
    return jnp.clip(values, -limit, limit).astype(kind)


def setup_inputs(seed: int = 0, part: int = 0) -> dict:
    keys = jax.random.split(jax.random.key(seed), 9)
    part_keys = jax.random.split(jax.random.fold_in(keys[8], part), 9)
    pair_left = normal_values(part_keys[0], (I, K, C), 1.0, 6.0, ((0, 8), (1, 16)))
    pair_right = normal_values(part_keys[1], (J, K, C), 1.0, 6.0, ((0, 16), (1, 8)))
    pair_middle = normal_values(part_keys[2], (I, J, C), 1.0, 6.0, ((0, 8), (1, 16)))
    cotangent = normal_values(part_keys[3], (I, J, C), 1.0, 6.0, ((0, 8), (1, 16)))
    left_weight = normal_values(keys[4], (C, 2 * CH), C ** -0.5, 0.5)
    right_weight = normal_values(keys[5], (C, 2 * CH), C ** -0.5, 0.5)
    gate_weight = normal_values(keys[6], (C, C), C ** -0.5, 0.5)
    output_weight = normal_values(keys[7], (CH, C), CH ** -0.5, 0.5)
    return {"pair_left": pair_left, "pair_right": pair_right, "pair_middle": pair_middle, "cotangent": cotangent, "left_weight": left_weight, "right_weight": right_weight, "gate_weight": gate_weight, "output_weight": output_weight}


epsilon = 1e-05

def normalize(field):
    values = field.astype(jnp.float32)
    centred = values - lax.optimization_barrier(jnp.mean(values, axis=-1, keepdims=True))
    inverse = lax.rsqrt(lax.optimization_barrier(jnp.mean(centred * centred, axis=-1, keepdims=True)) + epsilon)
    return (centred * inverse, inverse)

def normalize_back(normed, inverse, upstream):
    first = lax.optimization_barrier(jnp.mean(upstream, axis=-1, keepdims=True))
    second = lax.optimization_barrier(jnp.mean(upstream * normed, axis=-1, keepdims=True))
    return inverse * (upstream - first - normed * second)

def flat_dot(inputs, weight):
    flat = inputs.reshape(-1, inputs.shape[-1])
    result = jnp.dot(flat, weight, preferred_element_type=jnp.float32)
    return result.reshape(inputs.shape[:-1] + (weight.shape[1],))

def outer_sum(inputs, grads):
    flat_in = inputs.reshape(-1, inputs.shape[-1])
    flat_back = grads.reshape(-1, grads.shape[-1])
    return jnp.dot(flat_in.T, flat_back, preferred_element_type=jnp.float32)

def gated_project(inputs, weight):
    width = weight.shape[1] // 2
    mixed_cols = flat_dot(inputs, weight)
    linear = mixed_cols[..., :width]
    switch = jax.nn.sigmoid(mixed_cols[..., width:])
    return (switch * linear, switch, linear)

def gated_back(inputs, switch, linear, upstream, weight):
    back_linear = upstream * switch
    back_gate = upstream * linear * switch * (1.0 - switch)
    joined = jnp.concatenate([back_linear, back_gate], axis=-1).astype(jnp.bfloat16)
    return (outer_sum(inputs, joined), flat_dot(joined, weight.T))

def reference(pair_left, pair_right, pair_middle, cotangent, left_weight, right_weight, gate_weight, output_weight):
    left_norm, left_inverse = normalize(pair_left)
    left_input = left_norm.astype(jnp.bfloat16)
    left_act, left_switch, left_linear = gated_project(left_input, left_weight)
    left_slab = left_act.astype(jnp.bfloat16)
    right_norm, right_inverse = normalize(pair_right)
    right_input = right_norm.astype(jnp.bfloat16)
    right_act, right_switch, right_linear = gated_project(right_input, right_weight)
    right_slab = right_act.astype(jnp.bfloat16)
    triangle = jnp.einsum('ikc,jkc->ijc', left_slab.astype(jnp.float32), right_slab.astype(jnp.float32))
    tri_norm, tri_inverse = normalize(triangle)
    tri_input = tri_norm.astype(jnp.bfloat16)
    middle_norm, middle_inverse = normalize(pair_middle)
    middle_input = middle_norm.astype(jnp.bfloat16)
    gate = jax.nn.sigmoid(flat_dot(middle_input, gate_weight))
    head = flat_dot(tri_input, output_weight)
    update = (gate * head).astype(jnp.bfloat16)
    upstream = cotangent.astype(jnp.float32)
    head_back = (upstream * gate).astype(jnp.bfloat16)
    pre_back = (upstream * head * gate * (1.0 - gate)).astype(jnp.bfloat16)
    output_delta = outer_sum(tri_input, head_back)
    gate_delta = outer_sum(middle_input, pre_back)
    grad_middle = normalize_back(middle_norm, middle_inverse, flat_dot(pre_back, gate_weight.T)).astype(jnp.bfloat16)
    tri_back = normalize_back(tri_norm, tri_inverse, flat_dot(head_back, output_weight.T)).astype(jnp.bfloat16)

    def left_group(group, total):
        start = jnp.asarray(group, jnp.int32) * JD
        rows_back = lax.dynamic_slice_in_dim(tri_back, start, JD, 1).astype(jnp.float32)
        partner = lax.dynamic_slice_in_dim(right_slab, start, JD, 0).astype(jnp.float32)
        term = jnp.einsum('ijc,jkc->ikc', rows_back, partner)
        rounded = lax.optimization_barrier(term.astype(jnp.bfloat16))
        return total + rounded.astype(jnp.float32)
    left_back = lax.fori_loop(0, N_BLK, left_group, jnp.zeros((I, K, CH), jnp.float32))

    def right_group(group, total):
        start = jnp.asarray(group, jnp.int32) * ID
        rows_back = lax.dynamic_slice_in_dim(tri_back, start, ID, 0).astype(jnp.float32)
        partner = lax.dynamic_slice_in_dim(left_slab, start, ID, 0).astype(jnp.float32)
        term = jnp.einsum('ijc,ikc->jkc', rows_back, partner)
        rounded = lax.optimization_barrier(term.astype(jnp.bfloat16))
        return total + rounded.astype(jnp.float32)
    right_back = lax.fori_loop(0, N_ROWS, right_group, jnp.zeros((J, K, CH), jnp.float32))
    left_delta, left_up = gated_back(left_input, left_switch, left_linear, left_back, left_weight)
    right_delta, right_up = gated_back(right_input, right_switch, right_linear, right_back, right_weight)
    grad_left = normalize_back(left_norm, left_inverse, left_up).astype(jnp.bfloat16)
    grad_right = normalize_back(right_norm, right_inverse, right_up).astype(jnp.bfloat16)
    return (update, grad_left, grad_right, grad_middle, left_delta, right_delta, gate_delta, output_delta)
```

```python
import jax
import jax.numpy as jnp
from jax import lax
from jax.experimental import pallas as pl
from jax.experimental.pallas import tpu as pltpu
from jax.sharding import PartitionSpec as P

epsilon = 1e-05


def normalize(field):
    values = field.astype(jnp.float32)
    centred = values - jnp.mean(values, axis=-1, keepdims=True)
    inverse = lax.rsqrt(jnp.mean(centred * centred, axis=-1, keepdims=True) + epsilon)
    return (centred * inverse, inverse)


def normalize_back(normed, inverse, upstream):
    first = jnp.mean(upstream, axis=-1, keepdims=True)
    second = jnp.mean(upstream * normed, axis=-1, keepdims=True)
    return inverse * (upstream - first - normed * second)


def flat_dot(inputs, weight):
    flat = inputs.reshape(-1, inputs.shape[-1])
    result = jnp.dot(flat, weight, preferred_element_type=jnp.float32)
    return result.reshape(inputs.shape[:-1] + (weight.shape[1],))


def outer_sum(inputs, grads):
    flat_in = inputs.reshape(-1, inputs.shape[-1])
    flat_back = grads.reshape(-1, grads.shape[-1])
    return jnp.einsum("rc,rd->cd", flat_in, flat_back, preferred_element_type=jnp.float32)


def gated_project(inputs, weight):
    width = weight.shape[1] // 2
    mixed_cols = flat_dot(inputs, weight)
    linear = mixed_cols[..., :width]
    switch = jax.nn.sigmoid(mixed_cols[..., width:])
    return (switch * linear, switch, linear)


def gated_back(inputs, switch, linear, upstream, weight):
    back_linear = upstream * switch
    back_gate = upstream * linear * switch * (1.0 - switch)
    joined = jnp.concatenate([back_linear, back_gate], axis=-1).astype(jnp.bfloat16)
    input_term = jnp.einsum("...d,cd->...c", joined, weight, preferred_element_type=jnp.float32)
    return (outer_sum(inputs, joined), input_term)


def partner(index):
    return {"rows": index // 16, "blk": lax.rem(index, 16)}


def reduce_kernel(x_ref, o_ref, recv, total, sems):
    me = lax.axis_index("rows") * 16 + lax.axis_index("blk")
    barrier = pltpu.get_barrier_semaphore()

    def greet(o, c):
        p = lax.rem(me + o, 128)
        pl.semaphore_signal(barrier, inc=1, device_id=partner(p), device_id_type=pl.DeviceIdType.MESH)
        return c

    lax.fori_loop(1, 128, greet, 0)
    pl.semaphore_wait(barrier, 127)

    def scatter(o, c):
        p = lax.rem(me + o, 128)
        pltpu.make_async_remote_copy(
            src_ref=x_ref.at[p], dst_ref=recv.at[me], send_sem=sems.at[0], recv_sem=sems.at[1],
            device_id=partner(p), device_id_type=pl.DeviceIdType.MESH).start()
        return c

    lax.fori_loop(1, 128, scatter, 0)
    recv[pl.ds(me, 1)] = x_ref[pl.ds(me, 1)]
    done = pltpu.make_async_remote_copy(
        src_ref=x_ref.at[pl.ds(0, 127)], dst_ref=recv.at[pl.ds(0, 127)], send_sem=sems.at[0], recv_sem=sems.at[1],
        device_id=partner(lax.rem(me + 1, 128)), device_id_type=pl.DeviceIdType.MESH)
    done.wait_recv()
    done.wait_send()
    total[...] = jnp.sum(recv[...], axis=0)

    def spread(o, c):
        p = lax.rem(me + o, 128)
        pltpu.make_async_remote_copy(
            src_ref=total, dst_ref=o_ref.at[me], send_sem=sems.at[2], recv_sem=sems.at[3],
            device_id=partner(p), device_id_type=pl.DeviceIdType.MESH).start()
        return c

    lax.fori_loop(1, 128, spread, 0)
    o_ref[pl.ds(me, 1)] = total[...][None]
    done = pltpu.make_async_remote_copy(
        src_ref=x_ref.at[pl.ds(0, 127)], dst_ref=o_ref.at[pl.ds(0, 127)], send_sem=sems.at[2], recv_sem=sems.at[3],
        device_id=partner(lax.rem(me + 1, 128)), device_id_type=pl.DeviceIdType.MESH)
    done.wait_recv()
    done.wait_send()


def reduce_all(parts):
    flat = jnp.concatenate([p.reshape(-1) for p in parts]).reshape(128, -1, 128)
    total = pl.pallas_call(
        reduce_kernel,
        out_shape=jax.ShapeDtypeStruct(flat.shape, jnp.float32),
        in_specs=[pl.BlockSpec(memory_space=pltpu.VMEM)],
        out_specs=pl.BlockSpec(memory_space=pltpu.VMEM),
        scratch_shapes=[
            pltpu.VMEM(flat.shape, jnp.float32),
            pltpu.VMEM(flat.shape[1:], jnp.float32),
            pltpu.SemaphoreType.DMA((4,)),
        ],
        compiler_params=pltpu.CompilerParams(collective_id=0, has_side_effects=True),
    )(flat).reshape(-1)
    out, at = [], 0
    for p in parts:
        out.append(total[at:at + p.size].reshape(p.shape))
        at += p.size
    return out


def per_device(
    pair_left,
    pair_right,
    pair_middle,
    cotangent,
    left_weight,
    right_weight,
    gate_weight,
    output_weight,
):
    left_norm, left_inverse = normalize(pair_left)
    left_input = left_norm.astype(jnp.bfloat16)
    left_act, left_switch, left_linear = gated_project(left_input, left_weight)
    left_slab = left_act.astype(jnp.bfloat16)
    right_norm, right_inverse = normalize(pair_right)
    right_input = right_norm.astype(jnp.bfloat16)
    right_act, right_switch, right_linear = gated_project(right_input, right_weight)
    right_slab = right_act.astype(jnp.bfloat16)
    right_whole = lax.all_gather(right_slab, "rows", axis=1, tiled=True)
    left_whole = lax.all_gather(left_slab, "blk", axis=1, tiled=True)
    triangle = jnp.einsum(
        "ikc,jkc->ijc", left_whole, right_whole, preferred_element_type=jnp.float32
    )
    tri_norm, tri_inverse = normalize(triangle)
    tri_input = tri_norm.astype(jnp.bfloat16)
    middle_norm, middle_inverse = normalize(pair_middle)
    middle_input = middle_norm.astype(jnp.bfloat16)
    gate = jax.nn.sigmoid(flat_dot(middle_input, gate_weight))
    head = flat_dot(tri_input, output_weight)
    update = (gate * head).astype(jnp.bfloat16)
    upstream = cotangent.astype(jnp.float32)
    head_back = (upstream * gate).astype(jnp.bfloat16)
    pre_back = (upstream * head * gate * (1.0 - gate)).astype(jnp.bfloat16)
    output_part = outer_sum(tri_input, head_back)
    gate_part = outer_sum(middle_input, pre_back)
    middle_up = jnp.einsum("ijd,cd->ijc", pre_back, gate_weight, preferred_element_type=jnp.float32)
    grad_middle = normalize_back(middle_norm, middle_inverse, middle_up).astype(jnp.bfloat16)
    tri_up = jnp.einsum("ijd,cd->ijc", head_back, output_weight, preferred_element_type=jnp.float32)
    tri_back = normalize_back(tri_norm, tri_inverse, tri_up).astype(jnp.bfloat16)
    partner = right_whole
    left_sums = lax.psum_scatter(
        jnp.einsum("ijc,jkc->kic", tri_back, partner, preferred_element_type=jnp.float32).astype(
            jnp.bfloat16
        ),
        "blk",
        scatter_dimension=0,
        tiled=True,
    ).astype(jnp.float32)
    left_back = jnp.transpose(left_sums, (1, 0, 2))
    partner = left_whole
    right_sums = lax.psum_scatter(
        jnp.einsum("ijc,ikc->kjc", tri_back, partner, preferred_element_type=jnp.float32).astype(
            jnp.bfloat16
        ),
        "rows",
        scatter_dimension=0,
        tiled=True,
    ).astype(jnp.float32)
    right_back = jnp.transpose(right_sums, (1, 0, 2))
    left_part, left_up = gated_back(left_input, left_switch, left_linear, left_back, left_weight)
    right_part, right_up = gated_back(
        right_input, right_switch, right_linear, right_back, right_weight
    )
    grad_left = normalize_back(left_norm, left_inverse, left_up).astype(jnp.bfloat16)
    grad_right = normalize_back(right_norm, right_inverse, right_up).astype(jnp.bfloat16)
    left_delta, right_delta, gate_delta, output_delta = reduce_all(
        (left_part, right_part, gate_part, output_part)
    )
    return (
        update,
        grad_left,
        grad_right,
        grad_middle,
        left_delta,
        right_delta,
        gate_delta,
        output_delta,
    )


def solution(mesh):
    placed = (
        P(("rep", "rows"), "blk", None),
        P(("rep", "blk"), "rows", None),
        P(("rep", "rows"), "blk", None),
        P(("rep", "rows"), "blk", None),
        P(),
        P(),
        P(),
        P(),
    )
    return jax.shard_map(
        per_device,
        mesh=mesh,
        in_specs=placed,
        out_specs=(
            P(("rep", "rows"), "blk", None),
            P(("rep", "rows"), "blk", None),
            P(("rep", "blk"), "rows", None),
            P(("rep", "rows"), "blk", None),
            P("rep", None),
            P("rep", None),
            P("rep", None),
            P("rep", None),
        ),
        check_vma=False,
    )
```

```python
import jax
import jax.numpy as jnp
from jax import lax
from jax.experimental import pallas as pl
from jax.experimental.pallas import tpu as pltpu
from jax.sharding import PartitionSpec as P

epsilon = 1e-05
F32 = jnp.float32
BF16 = jnp.bfloat16
MESH = pl.DeviceIdType.MESH
N = 128


def partner(p):
    return {"rows": p // 16, "blk": lax.rem(p, 16)}


def rows_norm(x):
    centred = x - jnp.mean(x, axis=-1, keepdims=True)
    inverse = lax.rsqrt(jnp.mean(centred * centred, axis=-1, keepdims=True) + epsilon)
    return centred * inverse, inverse


def rows_back(normed, inverse, up):
    first = jnp.mean(up, axis=-1, keepdims=True)
    second = jnp.mean(up * normed, axis=-1, keepdims=True)
    return inverse * (up - first - normed * second)


def dot(a, b, ca, cb):
    return lax.dot_general(a, b, (((ca,), (cb,)), ((), ())), preferred_element_type=F32)


def swap2(a, b):
    low = lax.broadcasted_iota(jnp.int32, a.shape, 1) < 64
    return (
        jnp.where(low, a, pltpu.roll(b, 64, 1)),
        jnp.where(low, pltpu.roll(a, 64, 1), b),
    )


def swap4(xs):
    y0, y2 = swap2(xs[0], xs[2])
    y1, y3 = swap2(xs[1], xs[3])
    low = (lax.broadcasted_iota(jnp.int32, y0.shape, 1) & 32) == 0
    outs = []
    for a, b in ((y0, y1), (y2, y3)):
        outs.append(jnp.where(low, a, pltpu.roll(b, 32, 1)))
        outs.append(jnp.where(low, pltpu.roll(a, 96, 1), b))
    return outs


def rows_at(start, size, step):
    return pl.ds(pl.multiple_of(start, step), size)


def kernel(
    left_ref, right_ref, mid_ref, cot_ref, lw_ref, rw_ref, gw_ref, ow_ref,
    update_ref, gleft_ref, gright_ref, gmid_ref, dleft_ref, dright_ref, dgate_ref, dout_ref,
    wide, send_a, send_b, send_c, send_d, recv_a, recv_b, recv_c, recv_d,
    norm_l, norm_r, inv_l, inv_r, in_l, in_r, lin, sw,
    lwt, rwt, mid_norm, mid_inv, mid_t, gate, head_back, tri_in, tri_t,
    lt, rt, tri, tb, lb, rb,
    sums, late_sums, early_recv, late_recv, early_total, late_total, early_all, late_all,
    sems,
):
    me = lax.axis_index("rows") * 16 + lax.axis_index("blk")
    barrier = pltpu.get_barrier_semaphore()

    def copy(src, dst, k, p):
        return pltpu.make_async_remote_copy(
            src_ref=src, dst_ref=dst, send_sem=sems.at[2 * k], recv_sem=sems.at[2 * k + 1],
            device_id=partner(p), device_id_type=MESH)

    def greet(o, c):
        pl.semaphore_signal(
            barrier, inc=1, device_id=partner(lax.rem(me + o, N)), device_id_type=MESH)
        return c

    lax.fori_loop(1, N, greet, 0)

    def spread(send, recv, k):
        def step(o, c):
            p = lax.rem(me + o, N)
            send[p] = wide[rows_at(p * 16, 16, 16), :].astype(BF16)
            copy(send.at[p], recv.at[me], k, p).start()
            return c
        lax.fori_loop(1, N, step, 0)
        recv[me] = wide[rows_at(me * 16, 16, 16), :].astype(BF16)

    def batch(send, recv, k):
        return copy(send.at[pl.ds(0, N - 1)], recv.at[pl.ds(0, N - 1)], k, lax.rem(me + 1, N))

    def widen(recv):
        def step(t, c):
            wide[rows_at(t * 256, 256, 256), :] = (
                recv[rows_at(t * 16, 16, 16)].astype(F32).reshape(256, 128))
            return c
        lax.fori_loop(0, 8, step, 0)

    lwt[...] = lw_ref[...].astype(F32).T.astype(BF16)
    rwt[...] = rw_ref[...].astype(F32).T.astype(BF16)

    def norm_step(t, c):
        at = rows_at(t * 128, 128, 128)
        for ref, normed, inverse in ((left_ref, norm_l, inv_l), (right_ref, norm_r, inv_r)):
            n, i = rows_norm(ref[at, :].astype(F32))
            normed[at, :] = n
            inverse[at, :] = jnp.broadcast_to(i, n.shape)
        return c

    lax.fori_loop(0, 8, norm_step, 0)

    def chunk(ref, q, side):
        if side == 0:
            return jnp.concatenate([ref[pl.ds(q + 8 * h, 64, stride=16), :] for h in range(2)], axis=0)
        return jnp.concatenate([ref[pl.ds(q + 8 * h, 32, stride=32), :] for h in range(4)], axis=0)

    def project(q, c):
        for side, (normed, inputs, wt) in enumerate(((norm_l, in_l, lwt), (norm_r, in_r, rwt))):
            x = chunk(normed, q, side).astype(BF16)
            inputs[q] = x
            pre = dot(wt[...], x, 1, 1)
            linear, switch = pre[:N], jax.nn.sigmoid(pre[N:])
            lin[side * 8 + q] = linear
            sw[side * 8 + q] = switch
            wide[pl.ds(side * 8 + q, N, stride=16), :] = linear * switch
        return c

    lax.fori_loop(0, 8, project, 0)

    pl.semaphore_wait(barrier, N - 1)
    spread(send_a, recv_a, 0)

    def middle(s, c):
        x = mid_ref[:, s].astype(F32).reshape(N, 128)
        n, i = rows_norm(x)
        mid_norm[s] = n
        mid_inv[s] = jnp.broadcast_to(i, n.shape)
        mid_t[s] = n.T.astype(BF16)
        gate[s] = jax.nn.sigmoid(dot(n.astype(BF16), gw_ref[...], 1, 0))
        return c

    lax.fori_loop(0, 16, middle, 0)

    batch(send_a, recv_a, 0).wait_recv()

    def unpack_left(b, c):
        for h in range(4):
            e = recv_a[2 * h * 16 + b].astype(F32)[:8]
            o = recv_a[(2 * h + 1) * 16 + b].astype(F32)[:8]
            lt[rows_at(b * 16, 16, 16), h * 128:(h + 1) * 128] = (
                jnp.concatenate(swap2(e, o), axis=0).astype(BF16))
        return c

    def unpack_right(r, c):
        for g in range(4):
            outs = swap4([recv_a[r * 16 + 4 * g + t].astype(F32)[8:] for t in range(4)])
            rt[rows_at(r * 32, 32, 32), g * 128:(g + 1) * 128] = (
                jnp.concatenate(outs, axis=0).astype(BF16))
        return c

    lax.fori_loop(0, 16, unpack_left, 0)
    lax.fori_loop(0, 8, unpack_right, 0)
    for h in range(4):
        tri[h * 128:(h + 1) * 128, :] = dot(lt[:, h * 128:(h + 1) * 128], rt[...], 0, 0)

    def pack_tri(r, c):
        for g in range(4):
            outs = swap4([
                tri[rows_at(r * 64 + 16 * v, 16, 16), g * 128:(g + 1) * 128] for v in range(4)])
            for t in range(4):
                send_b[r * 16 + 4 * g + t] = outs[t].astype(BF16)
        return c

    lax.fori_loop(0, 8, pack_tri, 0)

    def send_tri(o, c):
        p = lax.rem(me + o, N)
        copy(send_b.at[p], recv_b.at[me], 1, p).start()
        return c

    lax.fori_loop(1, N, send_tri, 0)
    recv_b[me] = send_b[me]

    batch(send_b, recv_b, 1).wait_recv()
    widen(recv_b)

    def heads(s, c):
        at = pl.ds(s, N, stride=16)
        x = wide[at, :]
        centred = x - jnp.mean(x, axis=0, keepdims=True)
        inverse = lax.rsqrt(jnp.mean(centred * centred, axis=0, keepdims=True) + epsilon)
        normed = centred * inverse
        tri_in[s] = normed.astype(BF16)
        tri_t[s] = normed.T.astype(BF16)
        back = (cot_ref[:, s].astype(F32).reshape(N, 128) * gate[s]).astype(BF16)
        head_back[s] = back
        up = dot(ow_ref[...], back, 1, 1)
        first = jnp.mean(up, axis=0, keepdims=True)
        second = jnp.mean(up * normed, axis=0, keepdims=True)
        wide[at, :] = inverse * (up - first - normed * second)
        return c

    lax.fori_loop(0, 16, heads, 0)
    spread(send_c, recv_c, 2)

    sums[...] = jnp.zeros_like(sums)

    def rest(s, c):
        g = gate[s]
        h = dot(tri_t[s], ow_ref[...], 1, 0)
        update_ref[:, s] = (g * h).astype(BF16).reshape(4, 32, 128)
        back = (cot_ref[:, s].astype(F32).reshape(N, 128) * h * g * (1.0 - g)).astype(BF16)
        sums[0:128, :] += dot(mid_t[s], back, 1, 0)
        sums[128:256, :] += dot(tri_in[s], head_back[s], 1, 0)
        up = dot(back, gw_ref[...], 1, 1)
        gmid_ref[:, s] = rows_back(mid_norm[s], mid_inv[s], up).astype(BF16).reshape(4, 32, 128)
        return c

    lax.fori_loop(0, 16, rest, 0)

    def reduce_start(src, recv, k, low, count):
        def step(o, c):
            t = lax.rem(me + o, count)
            @pl.when(low + t != me)
            def _():
                copy(src.at[rows_at(t * 8, 8, 8)], recv.at[me], k, low + t).start()
            return c
        lax.fori_loop(0, count, step, 0)

    def mine(low, count):
        return jnp.logical_and(me >= low, me < low + count)

    def reduce_end(src, recv, total, whole, k, low, count):
        @pl.when(mine(low, count))
        def _():
            batch(recv, recv, k).wait_recv()
            recv[me] = src[rows_at((me - low) * 8, 8, 8), :]
            total[...] = jnp.sum(recv[...], axis=0)
            whole[rows_at((me - low) * 8, 8, 8), :] = total[...]

            def step(o, c):
                p = lax.rem(me + o, N)
                copy(total, whole.at[rows_at((me - low) * 8, 8, 8)], k + 1, p).start()
                return c

            lax.fori_loop(1, N, step, 0)

    def spread_end(recv, whole, k, low, count):
        part = pl.ds(0, (count - 1) * 8)
        @pl.when(mine(low, count))
        def _():
            copy(whole.at[part], whole.at[part], k + 1, lax.rem(me + 1, N)).wait_recv()
        @pl.when(jnp.logical_not(mine(low, count)))
        def _():
            copy(whole, whole, k + 1, lax.rem(me + 1, N)).wait_recv()

    def sends_end(src, recv, k, low, count):
        part = pl.ds(0, (count - 1) * 8)
        @pl.when(mine(low, count))
        def _():
            copy(src.at[part], src.at[part], k, lax.rem(me + 1, N)).wait_send()
            batch(recv, recv, k + 1).wait_send()
        @pl.when(jnp.logical_not(mine(low, count)))
        def _():
            copy(src, src, k, lax.rem(me + 1, N)).wait_send()

    reduce_start(sums, early_recv, 4, 64, 32)

    batch(send_c, recv_c, 2).wait_recv()

    def unpack_tb(r, c):
        for g in range(4):
            outs = swap4([recv_c[r * 16 + 4 * g + t].astype(F32) for t in range(4)])
            for v in range(4):
                tb[rows_at(r * 64 + 16 * v, 16, 16), g * 128:(g + 1) * 128] = outs[v].astype(BF16)
        return c

    lax.fori_loop(0, 8, unpack_tb, 0)
    for h in range(4):
        at = slice(h * 128, (h + 1) * 128)
        lb[:, at] = dot(rt[...], tb[at, :], 1, 1)
        rb[:, at] = dot(lt[...], tb[:, at], 1, 0)

    def pack_left(b, c):
        for h in range(4):
            tile = lb[rows_at(b * 16, 16, 16), h * 128:(h + 1) * 128]
            e, o = swap2(tile[:8], tile[8:])
            wide[rows_at((2 * h * 16 + b) * 16, 8, 8), :] = e
            wide[rows_at(((2 * h + 1) * 16 + b) * 16, 8, 8), :] = o
        return c

    def pack_right(r, c):
        for g in range(4):
            outs = swap4([
                rb[rows_at(r * 32 + 8 * v, 8, 8), g * 128:(g + 1) * 128] for v in range(4)])
            for t in range(4):
                wide[rows_at((r * 16 + 4 * g + t) * 16 + 8, 8, 8), :] = outs[t]
        return c

    lax.fori_loop(0, 16, pack_left, 0)
    lax.fori_loop(0, 8, pack_right, 0)
    spread(send_d, recv_d, 3)

    reduce_end(sums, early_recv, early_total, early_all, 4, 64, 32)

    batch(send_d, recv_d, 3).wait_recv()
    widen(recv_d)
    late_sums[...] = jnp.zeros_like(late_sums)

    def back_step(q, c):
        for side, (normed, inverse, inputs, w_ref) in enumerate(
                ((norm_l, inv_l, in_l, lw_ref), (norm_r, inv_r, in_r, rw_ref))):
            up = wide[pl.ds(side * 8 + q, N, stride=16), :]
            linear, switch = lin[side * 8 + q], sw[side * 8 + q]
            grads = jnp.concatenate(
                [up * switch, up * linear * switch * (1.0 - switch)], axis=0).astype(BF16)
            late_sums[side * 256:(side + 1) * 256, :] += dot(grads, inputs[q], 1, 0)
            input_up = dot(w_ref[...], grads, 1, 0).T
            out = rows_back(chunk(normed, q, side), chunk(inverse, q, side), input_up)
            if side == 0:
                for h in range(2):
                    norm_l[pl.ds(q + 8 * h, 64, stride=16), :] = out[h * 64:(h + 1) * 64]
            else:
                for h in range(4):
                    norm_r[pl.ds(q + 8 * h, 32, stride=32), :] = out[h * 32:(h + 1) * 32]
        return c

    lax.fori_loop(0, 8, back_step, 0)
    reduce_start(late_sums, late_recv, 6, 0, 64)

    def round_step(t, c):
        at = rows_at(t * 128, 128, 128)
        gleft_ref[at, :] = norm_l[at, :].astype(BF16)
        gright_ref[at, :] = norm_r[at, :].astype(BF16)
        return c

    lax.fori_loop(0, 8, round_step, 0)
    reduce_end(late_sums, late_recv, late_total, late_all, 6, 0, 64)
    spread_end(early_recv, early_all, 4, 64, 32)
    dgate_ref[...] = early_all[0:128, :]
    dout_ref[...] = early_all[128:256, :]
    spread_end(late_recv, late_all, 6, 0, 64)
    dleft_ref[...] = late_all[0:256, :].T
    dright_ref[...] = late_all[256:512, :].T

    for k, (send, recv) in enumerate(
            ((send_a, recv_a), (send_b, recv_b), (send_c, recv_c), (send_d, recv_d))):
        batch(send, recv, k).wait_send()
    sends_end(sums, early_recv, 4, 64, 32)
    sends_end(late_sums, late_recv, 6, 0, 64)


def per_device(left, right, middle, cotangent, lw, rw, gw, ow):
    tile = (N, 16, 128)
    scratch = (
        [((2048, 128), F32)] + [(tile, BF16)] * 8
        + [((1024, 128), F32)] * 4 + [((8, 128, 128), BF16)] * 2 + [((16, 128, 128), F32)] * 2
        + [((256, 128), BF16)] * 2 + [((16, 128, 128), F32)] * 2 + [((16, 128, 128), BF16)]
        + [((16, 128, 128), F32)] + [((16, 128, 128), BF16)] * 3
        + [((256, 512), BF16)] * 2 + [((512, 512), F32), ((512, 512), BF16)] + [((256, 512), F32)] * 2
        + [((256, 128), F32), ((512, 128), F32)] + [((N, 8, 128), F32)] * 2
        + [((8, 128), F32)] * 2 + [((256, 128), F32), ((512, 128), F32)]
    )
    vmem = pl.BlockSpec(memory_space=pltpu.VMEM)
    outs = pl.pallas_call(
        kernel,
        out_shape=[
            jax.ShapeDtypeStruct((4, 16, 32, 128), BF16),
            jax.ShapeDtypeStruct((1024, 128), BF16),
            jax.ShapeDtypeStruct((1024, 128), BF16),
            jax.ShapeDtypeStruct((4, 16, 32, 128), BF16),
            jax.ShapeDtypeStruct((128, 256), F32),
            jax.ShapeDtypeStruct((128, 256), F32),
            jax.ShapeDtypeStruct((128, 128), F32),
            jax.ShapeDtypeStruct((128, 128), F32),
        ],
        in_specs=[vmem] * 8,
        out_specs=[vmem] * 8,
        scratch_shapes=[pltpu.VMEM(s, t) for s, t in scratch] + [pltpu.SemaphoreType.DMA((16,))],
        compiler_params=pltpu.CompilerParams(
            collective_id=0, has_side_effects=True, vmem_limit_bytes=48 * 2**20),
    )(
        left.reshape(1024, 128), right.reshape(1024, 128),
        middle.reshape(4, 16, 32, 128), cotangent.reshape(4, 16, 32, 128), lw, rw, gw, ow,
    )
    return (
        outs[0].reshape(64, 32, 128), outs[1].reshape(64, 16, 128),
        outs[2].reshape(32, 32, 128), outs[3].reshape(64, 32, 128), *outs[4:],
    )


def solution(mesh):
    over_i = P(("rep", "rows"), "blk", None)
    over_j = P(("rep", "blk"), "rows", None)
    part = P("rep", None)
    return jax.shard_map(
        per_device,
        mesh=mesh,
        in_specs=(over_i, over_j, over_i, over_i, P(), P(), P(), P()),
        out_specs=(over_i, over_i, over_j, over_i, part, part, part, part),
        check_vma=False,
    )
```

```python
import jax
import jax.numpy as jnp
from jax import lax
from jax.experimental import pallas as pl
from jax.experimental.pallas import tpu as pltpu
from jax.sharding import PartitionSpec as P

epsilon = 1e-05
F32 = jnp.float32
BF16 = jnp.bfloat16
MESH = pl.DeviceIdType.MESH
N = 128


def partner(p):
    return {"rows": p // 16, "blk": lax.rem(p, 16)}


def rows_norm(x):
    centred = x - jnp.mean(x, axis=-1, keepdims=True)
    inverse = lax.rsqrt(jnp.mean(centred * centred, axis=-1, keepdims=True) + epsilon)
    return centred * inverse, inverse


def rows_back(normed, inverse, up):
    first = jnp.mean(up, axis=-1, keepdims=True)
    second = jnp.mean(up * normed, axis=-1, keepdims=True)
    return inverse * (up - first - normed * second)


def dot(a, b, ca, cb):
    return lax.dot_general(a, b, (((ca,), (cb,)), ((), ())), preferred_element_type=F32)


def swap2(a, b):
    low = lax.broadcasted_iota(jnp.int32, a.shape, 1) < 64
    return (
        jnp.where(low, a, pltpu.roll(b, 64, 1)),
        jnp.where(low, pltpu.roll(a, 64, 1), b),
    )


def swap4(xs):
    y0, y2 = swap2(xs[0], xs[2])
    y1, y3 = swap2(xs[1], xs[3])
    low = (lax.broadcasted_iota(jnp.int32, y0.shape, 1) & 32) == 0
    outs = []
    for a, b in ((y0, y1), (y2, y3)):
        outs.append(jnp.where(low, a, pltpu.roll(b, 32, 1)))
        outs.append(jnp.where(low, pltpu.roll(a, 96, 1), b))
    return outs


def rows_at(start, size, step):
    return pl.ds(pl.multiple_of(start, step), size)


def kernel(
    left_hbm, right_hbm, mid_hbm, cot_hbm, lw_hbm, rw_hbm, gw_hbm, ow_hbm,
    update_hbm, gleft_hbm, gright_hbm, gmid_hbm, dleft_hbm, dright_hbm, dgate_hbm, dout_hbm,
    update_ref, gleft_ref, gright_ref, gmid_ref, dleft_ref, dright_ref, dgate_ref, dout_ref,
    left_ref, right_ref, mid_ref, cot_ref, lw_ref, rw_ref, gw_ref, ow_ref,
    wide, send_a, send_b, send_c, send_d, recv_a, recv_b, recv_c, recv_d,
    norm_l, norm_r, inv_l, inv_r, in_l, in_r, lin, sw,
    lwt, rwt, mid_norm, mid_inv, mid_t, gate, head_back, tri_in, tri_t,
    lt, rt, tri, tb, lb, rb,
    grads_l, grads_r, sums, late_sums, early_send, late_send, early_recv, late_recv,
    early_total, late_total, early_all, late_all, sems, fetch_sems, store_sems,
):
    me = lax.axis_index("rows") * 16 + lax.axis_index("blk")
    barrier = pltpu.get_barrier_semaphore()
    fetches = [
        pltpu.make_async_copy(src, dst, fetch_sems.at[n]) for n, (src, dst) in enumerate((
            (left_hbm, left_ref), (right_hbm, right_ref), (lw_hbm, lw_ref), (rw_hbm, rw_ref),
            (mid_hbm, mid_ref), (gw_hbm, gw_ref), (cot_hbm, cot_ref), (ow_hbm, ow_ref)))]
    for fetch in fetches:
        fetch.start()
    stores = []

    def store(*pairs):
        for src, dst in pairs:
            stores.append(pltpu.make_async_copy(src, dst, store_sems.at[len(stores)]))
            stores[-1].start()

    def copy(src, dst, k, p):
        return pltpu.make_async_remote_copy(
            src_ref=src, dst_ref=dst, send_sem=sems.at[2 * k], recv_sem=sems.at[2 * k + 1],
            device_id=partner(p), device_id_type=MESH)

    def greet(o, c):
        pl.semaphore_signal(
            barrier, inc=1, device_id=partner(lax.rem(me + o, N)), device_id_type=MESH)
        return c

    lax.fori_loop(1, N, greet, 0)

    def spread(send, recv, k):
        def step(o, c):
            p = lax.rem(me + o, N)
            send[p] = wide[rows_at(p * 16, 16, 16), :].astype(BF16)
            copy(send.at[p], recv.at[me], k, p).start()
            return c
        lax.fori_loop(1, N, step, 0)
        recv[me] = wide[rows_at(me * 16, 16, 16), :].astype(BF16)

    def batch(send, recv, k):
        return copy(send.at[pl.ds(0, N - 1)], recv.at[pl.ds(0, N - 1)], k, lax.rem(me + 1, N))

    def widen(recv):
        def step(t, c):
            wide[rows_at(t * 256, 256, 256), :] = (
                recv[rows_at(t * 16, 16, 16)].astype(F32).reshape(256, 128))
            return c
        lax.fori_loop(0, 8, step, 0)

    for fetch in fetches[:4]:
        fetch.wait()
    lwt[...] = lw_ref[...].astype(F32).T.astype(BF16)
    rwt[...] = rw_ref[...].astype(F32).T.astype(BF16)

    def norm_step(t, c):
        at = rows_at(t * 128, 128, 128)
        for ref, normed, inverse in ((left_ref, norm_l, inv_l), (right_ref, norm_r, inv_r)):
            n, i = rows_norm(ref[at, :].astype(F32))
            normed[at, :] = n
            inverse[at, :] = jnp.broadcast_to(i, n.shape)
        return c

    lax.fori_loop(0, 8, norm_step, 0)

    def chunk(ref, q, side):
        if side == 0:
            return jnp.concatenate([ref[pl.ds(q + 8 * h, 64, stride=16), :] for h in range(2)], axis=0)
        return jnp.concatenate([ref[pl.ds(q + 8 * h, 32, stride=32), :] for h in range(4)], axis=0)

    def project(q, c):
        for side, (normed, inputs, wt) in enumerate(((norm_l, in_l, lwt), (norm_r, in_r, rwt))):
            x = chunk(normed, q, side).astype(BF16)
            inputs[q] = x
            pre = dot(wt[...], x, 1, 1)
            linear, switch = pre[:N], jax.nn.sigmoid(pre[N:])
            lin[side * 8 + q] = linear
            sw[side * 8 + q] = switch
            wide[pl.ds(side * 8 + q, N, stride=16), :] = linear * switch
        return c

    lax.fori_loop(0, 8, project, 0)

    pl.semaphore_wait(barrier, N - 1)
    spread(send_a, recv_a, 0)

    def middle(s, c):
        x = mid_ref[:, s].astype(F32).reshape(N, 128)
        n, i = rows_norm(x)
        mid_norm[s] = n
        mid_inv[s] = jnp.broadcast_to(i, n.shape)
        mid_t[s] = n.T.astype(BF16)
        gate[s] = jax.nn.sigmoid(dot(n.astype(BF16), gw_ref[...], 1, 0))
        return c

    for fetch in fetches[4:]:
        fetch.wait()
    lax.fori_loop(0, 16, middle, 0)

    batch(send_a, recv_a, 0).wait_recv()

    def unpack_left(b, c):
        for h in range(4):
            e = recv_a[2 * h * 16 + b].astype(F32)[:8]
            o = recv_a[(2 * h + 1) * 16 + b].astype(F32)[:8]
            lt[rows_at(b * 16, 16, 16), h * 128:(h + 1) * 128] = (
                jnp.concatenate(swap2(e, o), axis=0).astype(BF16))
        return c

    def unpack_right(r, c):
        for g in range(4):
            outs = swap4([recv_a[r * 16 + 4 * g + t].astype(F32)[8:] for t in range(4)])
            rt[rows_at(r * 32, 32, 32), g * 128:(g + 1) * 128] = (
                jnp.concatenate(outs, axis=0).astype(BF16))
        return c

    lax.fori_loop(0, 16, unpack_left, 0)
    lax.fori_loop(0, 8, unpack_right, 0)
    for h in range(4):
        tri[h * 128:(h + 1) * 128, :] = dot(lt[:, h * 128:(h + 1) * 128], rt[...], 0, 0)

    def pack_tri(r, c):
        for g in range(4):
            outs = swap4([
                tri[rows_at(r * 64 + 16 * v, 16, 16), g * 128:(g + 1) * 128] for v in range(4)])
            for t in range(4):
                send_b[r * 16 + 4 * g + t] = outs[t].astype(BF16)
        return c

    lax.fori_loop(0, 8, pack_tri, 0)

    def send_tri(o, c):
        p = lax.rem(me + o, N)
        copy(send_b.at[p], recv_b.at[me], 1, p).start()
        return c

    lax.fori_loop(1, N, send_tri, 0)
    recv_b[me] = send_b[me]

    batch(send_b, recv_b, 1).wait_recv()
    widen(recv_b)

    def heads(s, c):
        at = pl.ds(s, N, stride=16)
        x = wide[at, :]
        centred = x - jnp.mean(x, axis=0, keepdims=True)
        inverse = lax.rsqrt(jnp.mean(centred * centred, axis=0, keepdims=True) + epsilon)
        normed = centred * inverse
        tri_in[s] = normed.astype(BF16)
        tri_t[s] = normed.T.astype(BF16)
        back = (cot_ref[:, s].astype(F32).reshape(N, 128) * gate[s]).astype(BF16)
        head_back[s] = back
        up = dot(ow_ref[...], back, 1, 1)
        first = jnp.mean(up, axis=0, keepdims=True)
        second = jnp.mean(up * normed, axis=0, keepdims=True)
        wide[at, :] = inverse * (up - first - normed * second)
        return c

    lax.fori_loop(0, 16, heads, 0)
    spread(send_c, recv_c, 2)

    sums[...] = jnp.zeros_like(sums)

    def rest(s, c):
        g = gate[s]
        h = dot(tri_t[s], ow_ref[...], 1, 0)
        update_ref[:, s] = (g * h).astype(BF16).reshape(4, 32, 128)
        back = (cot_ref[:, s].astype(F32).reshape(N, 128) * h * g * (1.0 - g)).astype(BF16)
        sums[0:128, :] += dot(mid_t[s], back, 1, 0)
        sums[128:256, :] += dot(tri_in[s], head_back[s], 1, 0)
        up = dot(back, gw_ref[...], 1, 1)
        gmid_ref[:, s] = rows_back(mid_norm[s], mid_inv[s], up).astype(BF16).reshape(4, 32, 128)
        return c

    lax.fori_loop(0, 16, rest, 0)
    store((update_ref, update_hbm), (gmid_ref, gmid_hbm))

    def owned(step, base):
        place = lax.rem(me, step) - base
        return jnp.logical_and(place >= 0, place < 2), (me // step) * 2 + place

    def reduce_start(src, send, recv, k, step, base, count):
        send[...] = src[...].astype(BF16)

        def one(o, c):
            t = lax.rem(me // (N // count) + o, count)
            p = (t // 2) * step + base + lax.rem(t, 2)
            @pl.when(p != me)
            def _():
                copy(send.at[rows_at(t * 16, 16, 16)], recv.at[me], k, p).start()
            return c

        lax.fori_loop(0, count, one, 0)

    def reduce_end(send, recv, total, whole, k, step, base):
        owner, t = owned(step, base)
        @pl.when(owner)
        def _():
            at = rows_at(t * 16, 16, 16)
            batch(recv, recv, k).wait_recv()
            recv[me] = send[at, :]
            total[...] = jnp.sum(recv[...].astype(F32), axis=0).astype(BF16)
            whole[at, :] = total[...]

            def one(o, c):
                copy(total, whole.at[at], k + 1, lax.rem(me + o, N)).start()
                return c

            lax.fori_loop(1, N, one, 0)

    def by_owner(ref, k, step, base, count, wait):
        owner, _ = owned(step, base)
        for own, rows in ((owner, count * 16 - 16), (jnp.logical_not(owner), count * 16)):
            @pl.when(own)
            def _():
                wait(copy(ref.at[pl.ds(0, rows)], ref.at[pl.ds(0, rows)], k, lax.rem(me + 1, N)))

    def spread_end(whole, k, step, base, count):
        by_owner(whole, k + 1, step, base, count, lambda c: c.wait_recv())

    def sends_end(send, recv, k, step, base, count):
        by_owner(send, k, step, base, count, lambda c: c.wait_send())
        @pl.when(owned(step, base)[0])
        def _():
            batch(recv, recv, k + 1).wait_send()

    early, late = (16, 4), (8, 0)
    reduce_start(sums, early_send, early_recv, 4, *early, 16)

    batch(send_c, recv_c, 2).wait_recv()

    def unpack_tb(r, c):
        for g in range(4):
            outs = swap4([recv_c[r * 16 + 4 * g + t].astype(F32) for t in range(4)])
            for v in range(4):
                tb[rows_at(r * 64 + 16 * v, 16, 16), g * 128:(g + 1) * 128] = outs[v].astype(BF16)
        return c

    lax.fori_loop(0, 8, unpack_tb, 0)
    for h in range(4):
        at = slice(h * 128, (h + 1) * 128)
        lb[:, at] = dot(rt[...], tb[at, :], 1, 1)
        rb[:, at] = dot(lt[...], tb[:, at], 1, 0)

    def pack_left(b, c):
        for h in range(4):
            tile = lb[rows_at(b * 16, 16, 16), h * 128:(h + 1) * 128]
            e, o = swap2(tile[:8], tile[8:])
            wide[rows_at((2 * h * 16 + b) * 16, 8, 8), :] = e
            wide[rows_at(((2 * h + 1) * 16 + b) * 16, 8, 8), :] = o
        return c

    def pack_right(r, c):
        for g in range(4):
            outs = swap4([
                rb[rows_at(r * 32 + 8 * v, 8, 8), g * 128:(g + 1) * 128] for v in range(4)])
            for t in range(4):
                wide[rows_at((r * 16 + 4 * g + t) * 16 + 8, 8, 8), :] = outs[t]
        return c

    lax.fori_loop(0, 16, pack_left, 0)
    lax.fori_loop(0, 8, pack_right, 0)
    spread(send_d, recv_d, 3)

    reduce_end(early_send, early_recv, early_total, early_all, 4, *early)

    batch(send_d, recv_d, 3).wait_recv()
    widen(recv_d)
    late_sums[...] = jnp.zeros_like(late_sums)

    sides = ((norm_l, inv_l, in_l, lw_ref, grads_l), (norm_r, inv_r, in_r, rw_ref, grads_r))

    def pre_grads(q, c):
        for side, (_, _, inputs, _, grads) in enumerate(sides):
            up = wide[pl.ds(side * 8 + q, N, stride=16), :]
            linear, switch = lin[side * 8 + q], sw[side * 8 + q]
            joined = jnp.concatenate(
                [up * switch, up * linear * switch * (1.0 - switch)], axis=0).astype(BF16)
            grads[q] = joined
            late_sums[side * 256:(side + 1) * 256, :] += dot(joined, inputs[q], 1, 0)
        return c

    lax.fori_loop(0, 8, pre_grads, 0)
    reduce_start(late_sums, late_send, late_recv, 6, *late, 32)

    def back_step(q, c):
        for side, (normed, inverse, _, w_ref, grads) in enumerate(sides):
            input_up = dot(w_ref[...], grads[q], 1, 0).T
            out = rows_back(chunk(normed, q, side), chunk(inverse, q, side), input_up)
            if side == 0:
                for h in range(2):
                    norm_l[pl.ds(q + 8 * h, 64, stride=16), :] = out[h * 64:(h + 1) * 64]
            else:
                for h in range(4):
                    norm_r[pl.ds(q + 8 * h, 32, stride=32), :] = out[h * 32:(h + 1) * 32]
        return c

    lax.fori_loop(0, 8, back_step, 0)

    def round_step(t, c):
        at = rows_at(t * 128, 128, 128)
        gleft_ref[at, :] = norm_l[at, :].astype(BF16)
        gright_ref[at, :] = norm_r[at, :].astype(BF16)
        return c

    lax.fori_loop(0, 8, round_step, 0)
    store((gleft_ref, gleft_hbm), (gright_ref, gright_hbm))
    reduce_end(late_send, late_recv, late_total, late_all, 6, *late)
    spread_end(early_all, 4, *early, 16)
    dgate_ref[...] = early_all[0:128, :].astype(F32)
    dout_ref[...] = early_all[128:256, :].astype(F32)
    spread_end(late_all, 6, *late, 32)
    dleft_ref[...] = late_all[0:256, :].astype(F32).T
    dright_ref[...] = late_all[256:512, :].astype(F32).T
    store((dgate_ref, dgate_hbm), (dout_ref, dout_hbm), (dleft_ref, dleft_hbm), (dright_ref, dright_hbm))

    for k, (send, recv) in enumerate(
            ((send_a, recv_a), (send_b, recv_b), (send_c, recv_c), (send_d, recv_d))):
        batch(send, recv, k).wait_send()
    sends_end(early_send, early_recv, 4, *early, 16)
    sends_end(late_send, late_recv, 6, *late, 32)
    for one in stores:
        one.wait()


def store_kernel(*refs):
    sources, targets, held, sems = refs[:8], refs[8:16], refs[16:24], refs[24]
    reads = [pltpu.make_async_copy(s, h, sems.at[n]) for n, (s, h) in enumerate(zip(sources, held))]
    writes = [pltpu.make_async_copy(h, t, sems.at[8 + n]) for n, (h, t) in enumerate(zip(held, targets))]
    for read in reads:
        read.start()
    for read, write in zip(reads, writes):
        read.wait()
        write.start()
    for write in writes:
        write.wait()


def per_device(left, right, middle, cotangent, lw, rw, gw, ow):
    tile = (N, 16, 128)
    pairs, flat, mids = (1024, 128), ((1024, 128), BF16), ((4, 16, 32, 128), BF16)
    results = [mids, flat, flat, mids] + [((128, 256), F32)] * 2 + [((128, 128), F32)] * 2
    shapes = [jax.ShapeDtypeStruct(s, t) for s, t in results]
    scratch = (
        results + [flat, flat, mids, mids] + [((128, 256), BF16)] * 2 + [((128, 128), BF16)] * 2
        + [((2048, 128), F32)] + [(tile, BF16)] * 8
        + [(pairs, F32)] * 4 + [((8, 128, 128), BF16)] * 2 + [((16, 128, 128), F32)] * 2
        + [((256, 128), BF16)] * 2 + [((16, 128, 128), F32)] * 2 + [((16, 128, 128), BF16)]
        + [((16, 128, 128), F32)] + [((16, 128, 128), BF16)] * 3
        + [((256, 512), BF16)] * 2 + [((512, 512), F32), ((512, 512), BF16)] + [((256, 512), F32)] * 2
        + [((8, 256, 128), BF16)] * 2
        + [((256, 128), F32), ((512, 128), F32), ((256, 128), BF16), ((512, 128), BF16)]
        + [(tile, BF16)] * 2 + [((16, 128), BF16)] * 2 + [((256, 128), BF16), ((512, 128), BF16)]
    )
    outs = pl.pallas_call(
        kernel,
        out_shape=shapes,
        in_specs=[pl.BlockSpec(memory_space=pltpu.HBM)] * 8,
        out_specs=[pl.BlockSpec(memory_space=pltpu.HBM)] * 8,
        scratch_shapes=[pltpu.VMEM(s, t) for s, t in scratch] + [
            pltpu.SemaphoreType.DMA((16,)), pltpu.SemaphoreType.DMA((8,)), pltpu.SemaphoreType.DMA((8,))],
        compiler_params=pltpu.CompilerParams(
            collective_id=0, has_side_effects=True, vmem_limit_bytes=61 * 2**20),
    )(
        left.reshape(pairs), right.reshape(pairs),
        middle.reshape(mids[0]), cotangent.reshape(mids[0]), lw, rw, gw, ow,
    )
    outs = pl.pallas_call(
        store_kernel,
        out_shape=shapes,
        in_specs=[pl.BlockSpec(memory_space=pltpu.HBM)] * 8,
        out_specs=[pl.BlockSpec(memory_space=pltpu.HBM)] * 8,
        scratch_shapes=[pltpu.VMEM(s, t) for s, t in results] + [pltpu.SemaphoreType.DMA((16,))],
        compiler_params=pltpu.CompilerParams(vmem_limit_bytes=61 * 2**20),
    )(*outs)
    return (
        outs[0].reshape(64, 32, 128), outs[1].reshape(64, 16, 128),
        outs[2].reshape(32, 32, 128), outs[3].reshape(64, 32, 128), *outs[4:],
    )


def solution(mesh):
    over_i = P(("rep", "rows"), "blk", None)
    over_j = P(("rep", "blk"), "rows", None)
    part = P("rep", None)
    return jax.shard_map(
        per_device,
        mesh=mesh,
        in_specs=(over_i, over_j, over_i, over_i, P(), P(), P(), P()),
        out_specs=(over_i, over_i, over_j, over_i, part, part, part, part),
        check_vma=False,
    )
```

```python
import jax
import jax.numpy as jnp
from jax import lax
from jax.experimental import pallas as pl
from jax.experimental.pallas import tpu as pltpu
from jax.sharding import PartitionSpec as P

epsilon = 1e-05
F32 = jnp.float32
BF16 = jnp.bfloat16
MESH = pl.DeviceIdType.MESH
N = 128


def partner(p):
    return {"rows": p // 16, "blk": lax.rem(p, 16)}


def rows_norm(x):
    centred = x - jnp.mean(x, axis=-1, keepdims=True)
    inverse = lax.rsqrt(jnp.mean(centred * centred, axis=-1, keepdims=True) + epsilon)
    return centred * inverse, inverse


def rows_back(normed, inverse, up):
    first = jnp.mean(up, axis=-1, keepdims=True)
    second = jnp.mean(up * normed, axis=-1, keepdims=True)
    return inverse * (up - first - normed * second)


def dot(a, b, ca, cb):
    return lax.dot_general(a, b, (((ca,), (cb,)), ((), ())), preferred_element_type=F32)


def swap2(a, b):
    low = lax.broadcasted_iota(jnp.int32, a.shape, 1) < 64
    return (
        jnp.where(low, a, pltpu.roll(b, 64, 1)),
        jnp.where(low, pltpu.roll(a, 64, 1), b),
    )


def swap4(xs):
    y0, y2 = swap2(xs[0], xs[2])
    y1, y3 = swap2(xs[1], xs[3])
    low = (lax.broadcasted_iota(jnp.int32, y0.shape, 1) & 32) == 0
    outs = []
    for a, b in ((y0, y1), (y2, y3)):
        outs.append(jnp.where(low, a, pltpu.roll(b, 32, 1)))
        outs.append(jnp.where(low, pltpu.roll(a, 96, 1), b))
    return outs


def rows_at(start, size, step):
    return pl.ds(pl.multiple_of(start, step), size)


def kernel(
    left_hbm, right_hbm, mid_hbm, cot_hbm, lw_hbm, rw_hbm, gw_hbm, ow_hbm,
    update_hbm, gleft_hbm, gright_hbm, gmid_hbm, dleft_hbm, dright_hbm, dgate_hbm, dout_hbm,
    update_ref, gleft_ref, gright_ref, gmid_ref, dleft_ref, dright_ref, dgate_ref, dout_ref,
    left_ref, right_ref, mid_ref, cot_ref, lw_ref, rw_ref, gw_ref, ow_ref,
    wide, send_a, send_b, send_c, send_d, recv_a, recv_b, recv_c, recv_d,
    norm_l, norm_r, inv_l, inv_r, in_l, in_r, lin, sw,
    lwt, rwt, mid_norm, mid_inv, mid_t, gate, head_back, tri_in,
    lt, rt, tri, tb, lb, rb,
    grads_l, grads_r, sums, late_sums, early_send, late_send, early_held, late_held,
    early_part, late_part, early_parts, late_parts, early_all, late_all, sems, arrive_sems, fetch_sems, store_sems,
):
    my_row, my_blk = lax.axis_index("rows"), lax.axis_index("blk")
    me = my_row * 16 + my_blk
    barrier = pltpu.get_barrier_semaphore()
    fetches = [
        pltpu.make_async_copy(src, dst, fetch_sems.at[n]) for n, (src, dst) in enumerate((
            (left_hbm, left_ref), (right_hbm, right_ref), (lw_hbm, lw_ref), (rw_hbm, rw_ref),
            (mid_hbm, mid_ref), (gw_hbm, gw_ref), (cot_hbm, cot_ref), (ow_hbm, ow_ref)))]
    for fetch in fetches:
        fetch.start()
    stores = []

    def store(*pairs):
        for src, dst in pairs:
            stores.append(pltpu.make_async_copy(src, dst, store_sems.at[len(stores)]))
            stores[-1].start()

    def copy(src, dst, k, p, arrive=None):
        return pltpu.make_async_remote_copy(
            src_ref=src, dst_ref=dst, send_sem=sems.at[2 * k],
            recv_sem=sems.at[2 * k + 1] if arrive is None else arrive,
            device_id=partner(p), device_id_type=MESH)

    def greet(o, c):
        pl.semaphore_signal(
            barrier, inc=1, device_id=partner(lax.rem(me + o, N)), device_id_type=MESH)
        return c

    lax.fori_loop(1, N, greet, 0)

    def pair(g):
        return lax.rem(me // 32 + g, 4), lax.rem(me // 32 + 4 - g, 4)

    def spread(send, recv, k, fill=True):
        if fill:
            recv[me] = wide[rows_at(me * 16, 16, 16), :].astype(BF16)
        else:
            recv[me] = send[me]
        for g in range(4):
            def step(o, c):
                p = pair(g)[0] * 32 + lax.rem(me + o, 32)
                if fill:
                    send[p] = wide[rows_at(p * 16, 16, 16), :].astype(BF16)
                copy(send.at[p], recv.at[me], k, p, arrive_sems.at[4 * k + g]).start()
                return c
            lax.fori_loop(0 if g else 1, 32, step, 0)

    def arrived(recv, k, g):
        part = pl.ds(0, 32 if g else 31)
        copy(recv.at[part], recv.at[part], k, lax.rem(me + 1, N), arrive_sems.at[4 * k + g]).wait_recv()
        return pair(g)[1]

    def widen(recv, k):
        for g in range(4):
            first = arrived(recv, k, g) * 32
            def step(t, c):
                at = first + t * 16
                wide[rows_at(at * 16, 256, 256), :] = (
                    recv[rows_at(at, 16, 16)].astype(F32).reshape(256, 128))
                return c
            lax.fori_loop(0, 2, step, 0)

    for fetch in fetches[:4]:
        fetch.wait()
    lwt[...] = lw_ref[...].astype(F32).T.astype(BF16)
    rwt[...] = rw_ref[...].astype(F32).T.astype(BF16)

    def norm_step(t, c):
        at = rows_at(t * 128, 128, 128)
        for ref, normed, inverse in ((left_ref, norm_l, inv_l), (right_ref, norm_r, inv_r)):
            n, i = rows_norm(ref[at, :].astype(F32))
            normed[at, :] = n
            inverse[at, :] = jnp.broadcast_to(i, n.shape)
        return c

    lax.fori_loop(0, 8, norm_step, 0)

    def chunk(ref, q, side):
        if side == 0:
            return jnp.concatenate([ref[pl.ds(q + 8 * h, 64, stride=16), :] for h in range(2)], axis=0)
        return jnp.concatenate([ref[pl.ds(q + 8 * h, 32, stride=32), :] for h in range(4)], axis=0)

    def project(q, c):
        for side, (normed, inputs, wt) in enumerate(((norm_l, in_l, lwt), (norm_r, in_r, rwt))):
            x = chunk(normed, q, side).astype(BF16)
            inputs[q] = x
            pre = dot(wt[...], x, 1, 1)
            linear, switch = pre[:N], jax.nn.sigmoid(pre[N:])
            lin[side * 8 + q] = linear
            sw[side * 8 + q] = switch
            wide[pl.ds(side * 8 + q, N, stride=16), :] = linear * switch
        return c

    lax.fori_loop(0, 8, project, 0)

    pl.semaphore_wait(barrier, N - 1)
    spread(send_a, recv_a, 0)

    for g in range(4):
        h = arrived(recv_a, 0, g)
        at = rows_at(h * 128, 128, 128)

        def unpack_left(n, c):
            tiles = [[recv_a[h * 32 + 16 * v + n * 4 + u].astype(F32)[:8] for v in range(2)] for u in range(4)]
            outs = [out for e, o in tiles for out in swap2(e, o)]
            lt[rows_at(n * 64, 64, 64), at] = jnp.concatenate(outs, axis=0).astype(BF16)
            return c

        def unpack_right(n, c):
            r = h * 2 + n
            tiles = [recv_a[r * 16 + t].astype(F32)[8:] for t in range(16)]
            outs = [jnp.concatenate(swap4(tiles[4 * v:4 * v + 4]), axis=0) for v in range(4)]
            rt[rows_at(r * 32, 32, 32), :] = jnp.concatenate(outs, axis=1).astype(BF16)
            return c

        lax.fori_loop(0, 4, unpack_left, 0)
        lax.fori_loop(0, 2, unpack_right, 0)

    for h in range(4):
        tri[h * 128:(h + 1) * 128, :] = dot(lt[:, h * 128:(h + 1) * 128], rt[...], 0, 0)

    def pack_tri(r, c):
        rows = tri[rows_at(r * 64, 64, 64), :]
        outs = [swap4([rows[16 * v:16 * v + 16, g * 128:(g + 1) * 128] for v in range(4)]) for g in range(4)]
        for g in range(4):
            for t in range(4):
                send_b[r * 16 + 4 * g + t] = outs[g][t].astype(BF16)
        return c

    lax.fori_loop(0, 8, pack_tri, 0)

    spread(send_b, recv_b, 1, fill=False)

    def middle(q, c):
        slots = (2 * q, 2 * q + 1)
        xs = [mid_ref[:, s].astype(F32).reshape(N, 128) for s in slots]
        norms = [rows_norm(x) for x in xs]
        gates = [jax.nn.sigmoid(dot(n.astype(BF16), gw_ref[...], 1, 0)) for n, _ in norms]
        turned = [n.T.astype(BF16) for n, _ in norms]
        for s, (n, i), g, t in zip(slots, norms, gates, turned):
            mid_norm[s] = n
            mid_inv[s] = jnp.broadcast_to(i, n.shape)
            mid_t[s] = t
            gate[s] = g
        return c

    for fetch in fetches[4:]:
        fetch.wait()
    lax.fori_loop(0, 8, middle, 0)

    widen(recv_b, 1)

    def heads(q, c):
        slots = (2 * q, 2 * q + 1)
        at = [pl.ds(s, N, stride=16) for s in slots]
        xs = [wide[a, :] for a in at]
        backs = [(cot_ref[:, s].astype(F32).reshape(N, 128) * gate[s]).astype(BF16) for s in slots]
        ups = [dot(ow_ref[...], back, 1, 1) for back in backs]
        outs = []
        for x, up in zip(xs, ups):
            centred = x - jnp.mean(x, axis=0, keepdims=True)
            inverse = lax.rsqrt(jnp.mean(centred * centred, axis=0, keepdims=True) + epsilon)
            normed = centred * inverse
            first = jnp.mean(up, axis=0, keepdims=True)
            second = jnp.mean(up * normed, axis=0, keepdims=True)
            outs.append((normed, inverse * (up - first - normed * second)))
        for s, a, back, (normed, out) in zip(slots, at, backs, outs):
            head_back[s] = back
            tri_in[s] = normed.astype(BF16)
            wide[a, :] = out
        return c

    lax.fori_loop(0, 8, heads, 0)
    spread(send_c, recv_c, 2)

    def over_blk(o):
        return my_row * 16 + lax.rem(my_blk + o, 16)

    def sum_scatter(src, send, held, k):
        send[...] = src[...].astype(BF16)
        rows = held.shape[1]
        for o in range(1, 16):
            p = over_blk(o)
            at = rows_at(lax.rem(p, 16) * rows, rows, rows)
            copy(send.at[at], held.at[my_blk], k, p).start()
        held[my_blk] = send[rows_at(my_blk * rows, rows, rows), :]

    def sum_exchange(held, part, parts, k):
        copy(held.at[pl.ds(0, 15)], held.at[pl.ds(0, 15)], k, over_blk(1)).wait_recv()
        part[...] = jnp.sum(held[...].astype(F32), axis=0)
        for o in range(1, 8):
            copy(part, parts.at[my_row], k + 1, lax.rem(me + 16 * o, N)).start()
        parts[my_row] = part[...]

    def sum_spread(parts, whole, k):
        copy(parts.at[pl.ds(0, 7)], parts.at[pl.ds(0, 7)], k + 1, lax.rem(me + 16, N)).wait_recv()
        rows = parts.shape[1]
        at = rows_at(my_blk * rows, rows, rows)
        whole[at, :] = jnp.sum(parts[...], axis=0).astype(BF16)
        for o in range(1, 16):
            copy(whole.at[at], whole.at[at], k + 2, over_blk(o)).start()

    def sum_wait(whole, k):
        most = pl.ds(0, whole.shape[0] // 16 * 15)
        copy(whole.at[most], whole.at[most], k + 2, over_blk(1)).wait_recv()

    def sum_sent(whole, parts, k):
        most = pl.ds(0, whole.shape[0] // 16 * 15)
        copy(whole.at[most], whole.at[most], k, over_blk(1)).wait_send()
        copy(parts.at[pl.ds(0, 7)], parts.at[pl.ds(0, 7)], k + 1, over_blk(1)).wait_send()
        copy(whole.at[most], whole.at[most], k + 2, over_blk(1)).wait_send()

    for g in range(4):
        h = arrived(recv_c, 2, g)
        at = rows_at(h * 128, 128, 128)

        def unpack_tb(n, c):
            r = h * 2 + n
            tiles = [recv_c[r * 16 + t].astype(F32) for t in range(16)]
            outs = [jnp.concatenate(swap4(tiles[4 * v:4 * v + 4]), axis=0) for v in range(4)]
            tb[rows_at(r * 64, 64, 64), :] = jnp.concatenate(outs, axis=1).astype(BF16)
            return c

        lax.fori_loop(0, 2, unpack_tb, 0)
        lb[...] = dot(rt[...], tb[at, :], 1, 1)
        if g == 0:
            rb[...] = dot(lt[:, at], tb[at, :], 1, 0)
        else:
            rb[...] += dot(lt[:, at], tb[at, :], 1, 0)

        def pack_left(n, c):
            tiles = [lb[rows_at((n * 4 + u) * 16, 16, 16), :] for u in range(4)]
            outs = [swap2(tile[:8], tile[8:]) for tile in tiles]
            for u in range(4):
                for v in range(2):
                    wide[rows_at((h * 32 + 16 * v + n * 4 + u) * 16, 8, 8), :] = outs[u][v]
            return c

        lax.fori_loop(0, 4, pack_left, 0)

    def pack_right(r, c):
        rows = rb[rows_at(r * 32, 32, 32), :]
        outs = [swap4([rows[8 * v:8 * v + 8, g * 128:(g + 1) * 128] for v in range(4)]) for g in range(4)]
        for g in range(4):
            for t in range(4):
                wide[rows_at((r * 16 + 4 * g + t) * 16 + 8, 8, 8), :] = outs[g][t]
        return c

    lax.fori_loop(0, 8, pack_right, 0)
    spread(send_d, recv_d, 3)

    sums[...] = jnp.zeros_like(sums)

    def rest(q, c):
        slots = (2 * q, 2 * q + 1)
        gates = [gate[s] for s in slots]
        hs = [dot(tri_in[s].astype(F32).T.astype(BF16), ow_ref[...], 1, 0) for s in slots]
        backs = [
            (cot_ref[:, s].astype(F32).reshape(N, 128) * h * g * (1.0 - g)).astype(BF16)
            for s, h, g in zip(slots, hs, gates)]
        outs = [
            rows_back(mid_norm[s], mid_inv[s], dot(b, gw_ref[...], 1, 1)).astype(BF16)
            for s, b in zip(slots, backs)]
        gate_sum = [dot(mid_t[s], b, 1, 0) for s, b in zip(slots, backs)]
        out_sum = [dot(tri_in[s], head_back[s], 1, 0) for s in slots]
        sums[0:128, :] += gate_sum[0] + gate_sum[1]
        sums[128:256, :] += out_sum[0] + out_sum[1]
        for s, g, h, out in zip(slots, gates, hs, outs):
            update_ref[:, s] = (g * h).astype(BF16).reshape(4, 32, 128)
            gmid_ref[:, s] = out.reshape(4, 32, 128)
        return c

    lax.fori_loop(0, 8, rest, 0)
    store((update_ref, update_hbm), (gmid_ref, gmid_hbm))

    sum_scatter(sums, early_send, early_held, 4)


    widen(recv_d, 3)
    late_sums[...] = jnp.zeros_like(late_sums)

    sides = ((norm_l, inv_l, in_l, lw_ref, grads_l), (norm_r, inv_r, in_r, rw_ref, grads_r))

    def pre_grads(q, c):
        for side, (_, _, inputs, _, grads) in enumerate(sides):
            up = wide[pl.ds(side * 8 + q, N, stride=16), :]
            linear, switch = lin[side * 8 + q], sw[side * 8 + q]
            joined = jnp.concatenate(
                [up * switch, up * linear * switch * (1.0 - switch)], axis=0).astype(BF16)
            grads[q] = joined
            late_sums[side * 256:(side + 1) * 256, :] += dot(joined, inputs[q], 1, 0)
        return c

    lax.fori_loop(0, 8, pre_grads, 0)
    sum_scatter(late_sums, late_send, late_held, 7)
    sum_exchange(early_held, early_part, early_parts, 4)

    def back_step(q, c):
        outs = [
            rows_back(
                chunk(normed, q, side), chunk(inverse, q, side), dot(w_ref[...], grads[q], 1, 0).T)
            for side, (normed, inverse, _, w_ref, grads) in enumerate(sides)]
        for h in range(2):
            norm_l[pl.ds(q + 8 * h, 64, stride=16), :] = outs[0][h * 64:(h + 1) * 64]
        for h in range(4):
            norm_r[pl.ds(q + 8 * h, 32, stride=32), :] = outs[1][h * 32:(h + 1) * 32]
        return c

    lax.fori_loop(0, 8, back_step, 0)

    def round_step(t, c):
        at = rows_at(t * 128, 128, 128)
        gleft_ref[at, :] = norm_l[at, :].astype(BF16)
        gright_ref[at, :] = norm_r[at, :].astype(BF16)
        return c

    lax.fori_loop(0, 8, round_step, 0)
    store((gleft_ref, gleft_hbm), (gright_ref, gright_hbm))
    sum_exchange(late_held, late_part, late_parts, 7)
    sum_spread(early_parts, early_all, 4)
    sum_spread(late_parts, late_all, 7)
    sum_wait(early_all, 4)
    dgate_ref[...] = early_all[0:128, :].astype(F32)
    dout_ref[...] = early_all[128:256, :].astype(F32)
    sum_wait(late_all, 7)
    dleft_ref[...] = late_all[0:256, :].astype(F32).T
    dright_ref[...] = late_all[256:512, :].astype(F32).T
    store((dgate_ref, dgate_hbm), (dout_ref, dout_hbm), (dleft_ref, dleft_hbm), (dright_ref, dright_hbm))

    for k, send in enumerate((send_a, send_b, send_c, send_d)):
        most = send.at[pl.ds(0, N - 1)]
        copy(most, most, k, lax.rem(me + 1, N)).wait_send()
    sum_sent(early_all, early_parts, 4)
    sum_sent(late_all, late_parts, 7)
    for one in stores:
        one.wait()


def store_kernel(*refs):
    sources, targets, held, sems = refs[:8], refs[8:16], refs[16:24], refs[24]
    reads = [pltpu.make_async_copy(s, h, sems.at[n]) for n, (s, h) in enumerate(zip(sources, held))]
    writes = [pltpu.make_async_copy(h, t, sems.at[8 + n]) for n, (h, t) in enumerate(zip(held, targets))]
    for read in reads:
        read.start()
    for read, write in zip(reads, writes):
        read.wait()
        write.start()
    for write in writes:
        write.wait()


def per_device(left, right, middle, cotangent, lw, rw, gw, ow):
    tile = (N, 16, 128)
    pairs, flat, mids = (1024, 128), ((1024, 128), BF16), ((4, 16, 32, 128), BF16)
    results = [mids, flat, flat, mids] + [((128, 256), F32)] * 2 + [((128, 128), F32)] * 2
    shapes = [jax.ShapeDtypeStruct(s, t) for s, t in results]
    scratch = (
        results + [flat, flat, mids, mids] + [((128, 256), BF16)] * 2 + [((128, 128), BF16)] * 2
        + [((2048, 128), F32)] + [(tile, BF16)] * 8
        + [(pairs, F32)] * 4 + [((8, 128, 128), BF16)] * 2 + [((16, 128, 128), F32)] * 2
        + [((256, 128), BF16)] * 2 + [((16, 128, 128), F32)] * 2 + [((16, 128, 128), BF16)]
        + [((16, 128, 128), F32)] + [((16, 128, 128), BF16)] * 2
        + [((256, 512), BF16)] * 2 + [((512, 512), F32), ((512, 512), BF16)] + [((256, 128), F32), ((256, 512), F32)]
        + [((8, 256, 128), BF16)] * 2
        + [((256, 128), F32), ((512, 128), F32), ((256, 128), BF16), ((512, 128), BF16)]
        + [((16, 16, 128), BF16), ((16, 32, 128), BF16), ((16, 128), F32), ((32, 128), F32)]
        + [((8, 16, 128), F32), ((8, 32, 128), F32), ((256, 128), BF16), ((512, 128), BF16)]
    )
    outs = pl.pallas_call(
        kernel,
        out_shape=shapes,
        in_specs=[pl.BlockSpec(memory_space=pltpu.HBM)] * 8,
        out_specs=[pl.BlockSpec(memory_space=pltpu.HBM)] * 8,
        scratch_shapes=[pltpu.VMEM(s, t) for s, t in scratch] + [
            pltpu.SemaphoreType.DMA((20,)), pltpu.SemaphoreType.DMA((16,)), pltpu.SemaphoreType.DMA((8,)), pltpu.SemaphoreType.DMA((8,))],
        compiler_params=pltpu.CompilerParams(
            collective_id=0, has_side_effects=True, vmem_limit_bytes=61 * 2**20),
    )(
        left.reshape(pairs), right.reshape(pairs),
        middle.reshape(mids[0]), cotangent.reshape(mids[0]), lw, rw, gw, ow,
    )
    outs = pl.pallas_call(
        store_kernel,
        out_shape=shapes,
        in_specs=[pl.BlockSpec(memory_space=pltpu.HBM)] * 8,
        out_specs=[pl.BlockSpec(memory_space=pltpu.HBM)] * 8,
        scratch_shapes=[pltpu.VMEM(s, t) for s, t in results] + [pltpu.SemaphoreType.DMA((16,))],
        compiler_params=pltpu.CompilerParams(vmem_limit_bytes=61 * 2**20),
    )(*outs)
    return (
        outs[0].reshape(64, 32, 128), outs[1].reshape(64, 16, 128),
        outs[2].reshape(32, 32, 128), outs[3].reshape(64, 32, 128), *outs[4:],
    )


def solution(mesh):
    over_i = P(("rep", "rows"), "blk", None)
    over_j = P(("rep", "blk"), "rows", None)
    part = P("rep", None)
    return jax.shard_map(
        per_device,
        mesh=mesh,
        in_specs=(over_i, over_j, over_i, over_i, P(), P(), P(), P()),
        out_specs=(over_i, over_i, over_j, over_i, part, part, part, part),
        check_vma=False,
    )
```

```python
import jax
import jax.numpy as jnp
from jax import lax
from jax.experimental import pallas as pl
from jax.experimental.pallas import tpu as pltpu
from jax.sharding import PartitionSpec as P

epsilon = 1e-05
F32 = jnp.float32
BF16 = jnp.bfloat16
MESH = pl.DeviceIdType.MESH
N = 128


def partner(p):
    return {"rows": p // 16, "blk": lax.rem(p, 16)}


def rows_norm(x):
    centred = x - jnp.mean(x, axis=-1, keepdims=True)
    inverse = lax.rsqrt(jnp.mean(centred * centred, axis=-1, keepdims=True) + epsilon)
    return centred * inverse, inverse


def rows_back(normed, inverse, up):
    first = jnp.mean(up, axis=-1, keepdims=True)
    second = jnp.mean(up * normed, axis=-1, keepdims=True)
    return inverse * (up - first - normed * second)


def dot(a, b, ca, cb):
    return lax.dot_general(a, b, (((ca,), (cb,)), ((), ())), preferred_element_type=F32)


def swap2(a, b):
    low = lax.broadcasted_iota(jnp.int32, a.shape, 1) < 64
    return (
        jnp.where(low, a, pltpu.roll(b, 64, 1)),
        jnp.where(low, pltpu.roll(a, 64, 1), b),
    )


def swap4(xs):
    y0, y2 = swap2(xs[0], xs[2])
    y1, y3 = swap2(xs[1], xs[3])
    low = (lax.broadcasted_iota(jnp.int32, y0.shape, 1) & 32) == 0
    outs = []
    for a, b in ((y0, y1), (y2, y3)):
        outs.append(jnp.where(low, a, pltpu.roll(b, 32, 1)))
        outs.append(jnp.where(low, pltpu.roll(a, 96, 1), b))
    return outs


def rows_at(start, size, step):
    return pl.ds(pl.multiple_of(start, step), size)


def kernel(
    left_hbm, right_hbm, mid_hbm, cot_hbm, lw_hbm, rw_hbm, gw_hbm, ow_hbm,
    update_hbm, gleft_hbm, gright_hbm, gmid_hbm, dleft_hbm, dright_hbm, dgate_hbm, dout_hbm,
    update_ref, gleft_ref, gright_ref, gmid_ref, dleft_ref, dright_ref, dgate_ref, dout_ref,
    left_ref, right_ref, mid_ref, cot_ref, lw_ref, rw_ref, gw_ref, ow_ref,
    wide, send_a, send_b, send_c, send_d, recv_a, recv_b, recv_c, recv_d,
    norm_l, norm_r, inv_l, inv_r, in_l, in_r, lin, sw,
    lwt, rwt, mid_norm, mid_inv, mid_t, gate, head_back, tri_in,
    lt, rt, tri, tb, lb, rb,
    grads_l, grads_r, sums, late_sums, early_send, early_held, late_held,
    early_part, late_part, early_parts, late_parts, early_all, late_all, sems, arrive_sems, fetch_sems, store_sems,
):
    my_row, my_blk = lax.axis_index("rows"), lax.axis_index("blk")
    me = my_row * 16 + my_blk
    barrier = pltpu.get_barrier_semaphore()
    fetches = [
        pltpu.make_async_copy(src, dst, fetch_sems.at[n]) for n, (src, dst) in enumerate((
            (left_hbm, left_ref), (right_hbm, right_ref), (lw_hbm, lw_ref), (rw_hbm, rw_ref),
            (mid_hbm, mid_ref), (gw_hbm, gw_ref), (cot_hbm, cot_ref), (ow_hbm, ow_ref)))]
    for fetch in fetches:
        fetch.start()
    stores = []

    def store(*pairs):
        for src, dst in pairs:
            stores.append(pltpu.make_async_copy(src, dst, store_sems.at[len(stores)]))
            stores[-1].start()

    def copy(src, dst, k, p, arrive=None):
        return pltpu.make_async_remote_copy(
            src_ref=src, dst_ref=dst, send_sem=sems.at[2 * k],
            recv_sem=sems.at[2 * k + 1] if arrive is None else arrive,
            device_id=partner(p), device_id_type=MESH)

    def greet(o, c):
        pl.semaphore_signal(
            barrier, inc=1, device_id=partner(lax.rem(me + o, N)), device_id_type=MESH)
        return c

    lax.fori_loop(1, N, greet, 0)

    def pair(g):
        return lax.rem(me // 32 + g, 4), lax.rem(me // 32 + 4 - g, 4)

    def spread(send, recv, k, fill=True):
        if fill:
            recv[me] = wide[rows_at(me * 16, 16, 16), :].astype(BF16)
        else:
            recv[me] = send[me]
        for g in range(4):
            def step(o, c):
                p = pair(g)[0] * 32 + lax.rem(me + o, 32)
                if fill:
                    send[p] = wide[rows_at(p * 16, 16, 16), :].astype(BF16)
                copy(send.at[p], recv.at[me], k, p, arrive_sems.at[4 * k + g]).start()
                return c
            lax.fori_loop(0 if g else 1, 32, step, 0)

    def arrived(recv, k, g):
        part = pl.ds(0, 32 if g else 31)
        copy(recv.at[part], recv.at[part], k, lax.rem(me + 1, N), arrive_sems.at[4 * k + g]).wait_recv()
        return pair(g)[1]

    def widen_part(recv, h):
        def step(t, c):
            at = h * 32 + t * 16
            wide[rows_at(at * 16, 256, 256), :] = (
                recv[rows_at(at, 16, 16)].astype(F32).reshape(256, 128))
            return c
        lax.fori_loop(0, 2, step, 0)

    def widen(recv, k):
        for g in range(4):
            widen_part(recv, arrived(recv, k, g))

    for fetch in fetches[:4]:
        fetch.wait()
    lwt[...] = lw_ref[...].astype(F32).T.astype(BF16)
    rwt[...] = rw_ref[...].astype(F32).T.astype(BF16)

    def norm_step(t, c):
        at = rows_at(t * 128, 128, 128)
        for ref, normed, inverse in ((left_ref, norm_l, inv_l), (right_ref, norm_r, inv_r)):
            n, i = rows_norm(ref[at, :].astype(F32))
            normed[at, :] = n
            inverse[at, :] = jnp.broadcast_to(i, n.shape)
        return c

    lax.fori_loop(0, 8, norm_step, 0)

    def chunk(ref, q, side):
        if side == 0:
            return jnp.concatenate([ref[pl.ds(q + 8 * h, 64, stride=16), :] for h in range(2)], axis=0)
        return jnp.concatenate([ref[pl.ds(q + 8 * h, 32, stride=32), :] for h in range(4)], axis=0)

    def project(q, c):
        for side, (normed, inputs, wt) in enumerate(((norm_l, in_l, lwt), (norm_r, in_r, rwt))):
            x = chunk(normed, q, side).astype(BF16)
            inputs[q] = x
            pre = dot(wt[...], x, 1, 1)
            linear, switch = pre[:N], jax.nn.sigmoid(pre[N:])
            lin[side * 8 + q] = linear
            sw[side * 8 + q] = switch
            wide[pl.ds(side * 8 + q, N, stride=16), :] = linear * switch
        return c

    lax.fori_loop(0, 8, project, 0)

    pl.semaphore_wait(barrier, N - 1)
    spread(send_a, recv_a, 0)

    for g in range(4):
        h = arrived(recv_a, 0, g)
        at = rows_at(h * 128, 128, 128)

        def unpack_left(n, c):
            tiles = [[recv_a[h * 32 + 16 * v + n * 4 + u].astype(F32)[:8] for v in range(2)] for u in range(4)]
            outs = [out for e, o in tiles for out in swap2(e, o)]
            lt[rows_at(n * 64, 64, 64), at] = jnp.concatenate(outs, axis=0).astype(BF16)
            return c

        def unpack_right(n, c):
            r = h * 2 + n
            tiles = [recv_a[r * 16 + t].astype(F32)[8:] for t in range(16)]
            outs = [jnp.concatenate(swap4(tiles[4 * v:4 * v + 4]), axis=0) for v in range(4)]
            rt[rows_at(r * 32, 32, 32), :] = jnp.concatenate(outs, axis=1).astype(BF16)
            return c

        lax.fori_loop(0, 4, unpack_left, 0)
        lax.fori_loop(0, 2, unpack_right, 0)

    for h in range(4):
        tri[h * 128:(h + 1) * 128, :] = dot(lt[:, h * 128:(h + 1) * 128], rt[...], 0, 0)

    def pack_tri(r, c):
        rows = tri[rows_at(r * 64, 64, 64), :]
        outs = [swap4([rows[16 * v:16 * v + 16, g * 128:(g + 1) * 128] for v in range(4)]) for g in range(4)]
        for g in range(4):
            for t in range(4):
                send_b[r * 16 + 4 * g + t] = outs[g][t].astype(BF16)
        return c

    lax.fori_loop(0, 8, pack_tri, 0)

    spread(send_b, recv_b, 1, fill=False)

    def middle(q, c):
        slots = (2 * q, 2 * q + 1)
        xs = [mid_ref[:, s].astype(F32).reshape(N, 128) for s in slots]
        norms = [rows_norm(x) for x in xs]
        gates = [jax.nn.sigmoid(dot(n.astype(BF16), gw_ref[...], 1, 0)) for n, _ in norms]
        turned = [n.T.astype(BF16) for n, _ in norms]
        for s, (n, i), g, t in zip(slots, norms, gates, turned):
            mid_norm[s] = n
            mid_inv[s] = jnp.broadcast_to(i, n.shape)
            mid_t[s] = t
            gate[s] = g
        return c

    for fetch in fetches[4:]:
        fetch.wait()
    lax.fori_loop(0, 8, middle, 0)

    widen(recv_b, 1)

    def heads(q, c):
        slots = (2 * q, 2 * q + 1)
        at = [pl.ds(s, N, stride=16) for s in slots]
        xs = [wide[a, :] for a in at]
        backs = [(cot_ref[:, s].astype(F32).reshape(N, 128) * gate[s]).astype(BF16) for s in slots]
        ups = [dot(ow_ref[...], back, 1, 1) for back in backs]
        outs = []
        for x, up in zip(xs, ups):
            centred = x - jnp.mean(x, axis=0, keepdims=True)
            inverse = lax.rsqrt(jnp.mean(centred * centred, axis=0, keepdims=True) + epsilon)
            normed = centred * inverse
            first = jnp.mean(up, axis=0, keepdims=True)
            second = jnp.mean(up * normed, axis=0, keepdims=True)
            outs.append((normed, inverse * (up - first - normed * second)))
        for s, a, back, (normed, out) in zip(slots, at, backs, outs):
            head_back[s] = back
            tri_in[s] = normed.astype(BF16)
            wide[a, :] = out
        return c

    lax.fori_loop(0, 8, heads, 0)
    spread(send_c, recv_c, 2)

    def over_blk(o):
        return my_row * 16 + lax.rem(my_blk + o, 16)

    def sum_scatter(src, send, held, k):
        send[...] = src[...].astype(BF16)
        rows = held.shape[1]
        for o in range(1, 16):
            p = over_blk(o)
            at = rows_at(lax.rem(p, 16) * rows, rows, rows)
            copy(send.at[at], held.at[my_blk], k, p).start()
        held[my_blk] = send[rows_at(my_blk * rows, rows, rows), :]

    def sum_exchange(held, part, parts, k):
        slots = held.shape[0] // 16
        most = held.at[pl.ds(0, 15 * slots)]
        copy(most, most, k, over_blk(1)).wait_recv()
        part[...] = jnp.concatenate(
            [jnp.sum(held[16 * n:16 * n + 16].astype(F32), axis=0) for n in range(slots)], axis=0)
        for o in range(1, 8):
            copy(part, parts.at[my_row], k + 1, lax.rem(me + 16 * o, N)).start()
        parts[my_row] = part[...]

    def sum_spread(parts, whole, k):
        copy(parts.at[pl.ds(0, 7)], parts.at[pl.ds(0, 7)], k + 1, lax.rem(me + 16, N)).wait_recv()
        rows = parts.shape[1]
        at = rows_at(my_blk * rows, rows, rows)
        whole[at, :] = jnp.sum(parts[...], axis=0).astype(BF16)
        for o in range(1, 16):
            copy(whole.at[at], whole.at[at], k + 2, over_blk(o)).start()

    def sum_wait(whole, k):
        most = pl.ds(0, whole.shape[0] // 16 * 15)
        copy(whole.at[most], whole.at[most], k + 2, over_blk(1)).wait_recv()

    def sum_sent(held, whole, parts, k):
        most = held.at[pl.ds(0, held.shape[0] // 16 * 15)]
        copy(most, most, k, over_blk(1)).wait_send()
        most = pl.ds(0, whole.shape[0] // 16 * 15)
        copy(parts.at[pl.ds(0, 7)], parts.at[pl.ds(0, 7)], k + 1, over_blk(1)).wait_send()
        copy(whole.at[most], whole.at[most], k + 2, over_blk(1)).wait_send()

    for g in range(4):
        h = arrived(recv_c, 2, g)
        at = rows_at(h * 128, 128, 128)

        def unpack_tb(n, c):
            r = h * 2 + n
            tiles = [recv_c[r * 16 + t].astype(F32) for t in range(16)]
            outs = [jnp.concatenate(swap4(tiles[4 * v:4 * v + 4]), axis=0) for v in range(4)]
            tb[rows_at(r * 64, 64, 64), :] = jnp.concatenate(outs, axis=1).astype(BF16)
            return c

        lax.fori_loop(0, 2, unpack_tb, 0)
        lb[...] = dot(rt[...], tb[at, :], 1, 1)
        if g == 0:
            rb[...] = dot(lt[:, at], tb[at, :], 1, 0)
        else:
            rb[...] += dot(lt[:, at], tb[at, :], 1, 0)

        def pack_left(n, c):
            tiles = [lb[rows_at((n * 4 + u) * 16, 16, 16), :] for u in range(4)]
            outs = [swap2(tile[:8], tile[8:]) for tile in tiles]
            for u in range(4):
                for v in range(2):
                    wide[rows_at((h * 32 + 16 * v + n * 4 + u) * 16, 8, 8), :] = outs[u][v]
            return c

        lax.fori_loop(0, 4, pack_left, 0)

    def pack_right(r, c):
        rows = rb[rows_at(r * 32, 32, 32), :]
        outs = [swap4([rows[8 * v:8 * v + 8, g * 128:(g + 1) * 128] for v in range(4)]) for g in range(4)]
        for g in range(4):
            for t in range(4):
                wide[rows_at((r * 16 + 4 * g + t) * 16 + 8, 8, 8), :] = outs[g][t]
        return c

    lax.fori_loop(0, 8, pack_right, 0)
    spread(send_d, recv_d, 3)

    sums[...] = jnp.zeros_like(sums)

    def rest(q, c):
        slots = (2 * q, 2 * q + 1)
        gates = [gate[s] for s in slots]
        hs = [dot(tri_in[s].astype(F32).T.astype(BF16), ow_ref[...], 1, 0) for s in slots]
        backs = [
            (cot_ref[:, s].astype(F32).reshape(N, 128) * h * g * (1.0 - g)).astype(BF16)
            for s, h, g in zip(slots, hs, gates)]
        outs = [
            rows_back(mid_norm[s], mid_inv[s], dot(b, gw_ref[...], 1, 1)).astype(BF16)
            for s, b in zip(slots, backs)]
        gate_sum = [dot(mid_t[s], b, 1, 0) for s, b in zip(slots, backs)]
        out_sum = [dot(tri_in[s], head_back[s], 1, 0) for s in slots]
        sums[0:128, :] += gate_sum[0] + gate_sum[1]
        sums[128:256, :] += out_sum[0] + out_sum[1]
        for s, g, h, out in zip(slots, gates, hs, outs):
            update_ref[:, s] = (g * h).astype(BF16).reshape(4, 32, 128)
            gmid_ref[:, s] = out.reshape(4, 32, 128)
        return c

    lax.fori_loop(0, 8, rest, 0)
    store((update_ref, update_hbm), (gmid_ref, gmid_hbm))

    sum_scatter(sums, early_send, early_held, 4)


    sides = ((norm_l, inv_l, in_l, lw_ref, grads_l), (norm_r, inv_r, in_r, rw_ref, grads_r))
    for g in range(4):
        h = arrived(recv_d, 3, g)
        widen_part(recv_d, h)
        low = rows_at(h * 32, 32, 32)
        high = rows_at(h * 32 + 128, 32, 32)
        for side, (_, _, inputs, _, grads) in enumerate(sides):
            ups, switches = [], []
            for q in range(8):
                up = wide[pl.ds(h * 512 + side * 8 + q, 32, stride=16), :]
                linear, switch = lin[side * 8 + q, low, :], sw[side * 8 + q, low, :]
                ups.append((up * switch).astype(BF16))
                switches.append((up * linear * switch * (1.0 - switch)).astype(BF16))
                grads[q, low, :] = ups[q]
                grads[q, high, :] = switches[q]
            joined = jnp.concatenate(
                [jnp.concatenate(ups, axis=1), jnp.concatenate(switches, axis=1)], axis=0)
            late_sums[rows_at(h * 128 + side * 64, 64, 64), :] = dot(
                joined, inputs[...].reshape(1024, 128), 1, 0)
        for o in range(1, 16):
            p = over_blk(o)
            piece = rows_at(h * 128 + lax.rem(p, 16) * 8, 8, 8)
            copy(late_sums.at[piece], late_held.at[h * 16 + my_blk], 7, p).start()
        late_held[h * 16 + my_blk] = late_sums[rows_at(h * 128 + my_blk * 8, 8, 8), :]
    sum_exchange(early_held, early_part, early_parts, 4)

    def back_step(q, c):
        outs = [
            rows_back(
                chunk(normed, q, side), chunk(inverse, q, side), dot(w_ref[...], grads[q], 1, 0).T)
            for side, (normed, inverse, _, w_ref, grads) in enumerate(sides)]
        for h in range(2):
            norm_l[pl.ds(q + 8 * h, 64, stride=16), :] = outs[0][h * 64:(h + 1) * 64]
        for h in range(4):
            norm_r[pl.ds(q + 8 * h, 32, stride=32), :] = outs[1][h * 32:(h + 1) * 32]
        return c

    lax.fori_loop(0, 8, back_step, 0)

    def round_step(t, c):
        at = rows_at(t * 128, 128, 128)
        gleft_ref[at, :] = norm_l[at, :].astype(BF16)
        gright_ref[at, :] = norm_r[at, :].astype(BF16)
        return c

    lax.fori_loop(0, 8, round_step, 0)
    store((gleft_ref, gleft_hbm), (gright_ref, gright_hbm))
    sum_exchange(late_held, late_part, late_parts, 7)
    sum_spread(early_parts, early_all, 4)
    sum_spread(late_parts, late_all, 7)
    sum_wait(early_all, 4)
    dgate_ref[...] = early_all[0:128, :].astype(F32)
    dout_ref[...] = early_all[128:256, :].astype(F32)
    sum_wait(late_all, 7)
    whole = late_all[...].astype(F32)
    for side, target in enumerate((dleft_ref, dright_ref)):
        target[...] = jnp.concatenate([
            whole[b * 32 + h * 8:b * 32 + h * 8 + 8]
            for kind in range(2) for h in range(4)
            for b in range(side * 8 + kind * 4, side * 8 + kind * 4 + 4)], axis=0).T
    store((dgate_ref, dgate_hbm), (dout_ref, dout_hbm), (dleft_ref, dleft_hbm), (dright_ref, dright_hbm))

    for k, send in enumerate((send_a, send_b, send_c, send_d)):
        most = send.at[pl.ds(0, N - 1)]
        copy(most, most, k, lax.rem(me + 1, N)).wait_send()
    sum_sent(early_held, early_all, early_parts, 4)
    sum_sent(late_held, late_all, late_parts, 7)
    for one in stores:
        one.wait()


def store_kernel(*refs):
    sources, targets, held, sems = refs[:8], refs[8:16], refs[16:24], refs[24]
    reads = [pltpu.make_async_copy(s, h, sems.at[n]) for n, (s, h) in enumerate(zip(sources, held))]
    writes = [pltpu.make_async_copy(h, t, sems.at[8 + n]) for n, (h, t) in enumerate(zip(held, targets))]
    for read in reads:
        read.start()
    for read, write in zip(reads, writes):
        read.wait()
        write.start()
    for write in writes:
        write.wait()


def per_device(left, right, middle, cotangent, lw, rw, gw, ow):
    tile = (N, 16, 128)
    pairs, flat, mids = (1024, 128), ((1024, 128), BF16), ((4, 16, 32, 128), BF16)
    results = [mids, flat, flat, mids] + [((128, 256), F32)] * 2 + [((128, 128), F32)] * 2
    shapes = [jax.ShapeDtypeStruct(s, t) for s, t in results]
    scratch = (
        results + [flat, flat, mids, mids] + [((128, 256), BF16)] * 2 + [((128, 128), BF16)] * 2
        + [((2048, 128), F32)] + [(tile, BF16)] * 8
        + [(pairs, F32)] * 4 + [((8, 128, 128), BF16)] * 2 + [((16, 128, 128), F32)] * 2
        + [((256, 128), BF16)] * 2 + [((16, 128, 128), F32)] * 2 + [((16, 128, 128), BF16)]
        + [((16, 128, 128), F32)] + [((16, 128, 128), BF16)] * 2
        + [((256, 512), BF16)] * 2 + [((512, 512), F32), ((512, 512), BF16)] + [((256, 128), F32), ((256, 512), F32)]
        + [((8, 256, 128), BF16)] * 2
        + [((256, 128), F32), ((512, 128), F32), ((256, 128), BF16)]
        + [((16, 16, 128), BF16), ((64, 8, 128), F32), ((16, 128), F32), ((32, 128), F32)]
        + [((8, 16, 128), F32), ((8, 32, 128), F32), ((256, 128), BF16), ((512, 128), BF16)]
    )
    outs = pl.pallas_call(
        kernel,
        out_shape=shapes,
        in_specs=[pl.BlockSpec(memory_space=pltpu.HBM)] * 8,
        out_specs=[pl.BlockSpec(memory_space=pltpu.HBM)] * 8,
        scratch_shapes=[pltpu.VMEM(s, t) for s, t in scratch] + [
            pltpu.SemaphoreType.DMA((20,)), pltpu.SemaphoreType.DMA((16,)), pltpu.SemaphoreType.DMA((8,)), pltpu.SemaphoreType.DMA((8,))],
        compiler_params=pltpu.CompilerParams(
            collective_id=0, has_side_effects=True, vmem_limit_bytes=61 * 2**20),
    )(
        left.reshape(pairs), right.reshape(pairs),
        middle.reshape(mids[0]), cotangent.reshape(mids[0]), lw, rw, gw, ow,
    )
    outs = pl.pallas_call(
        store_kernel,
        out_shape=shapes,
        in_specs=[pl.BlockSpec(memory_space=pltpu.HBM)] * 8,
        out_specs=[pl.BlockSpec(memory_space=pltpu.HBM)] * 8,
        scratch_shapes=[pltpu.VMEM(s, t) for s, t in results] + [pltpu.SemaphoreType.DMA((16,))],
        compiler_params=pltpu.CompilerParams(vmem_limit_bytes=61 * 2**20),
    )(*outs)
    return (
        outs[0].reshape(64, 32, 128), outs[1].reshape(64, 16, 128),
        outs[2].reshape(32, 32, 128), outs[3].reshape(64, 32, 128), *outs[4:],
    )


def solution(mesh):
    over_i = P(("rep", "rows"), "blk", None)
    over_j = P(("rep", "blk"), "rows", None)
    part = P("rep", None)
    return jax.shard_map(
        per_device,
        mesh=mesh,
        in_specs=(over_i, over_j, over_i, over_i, P(), P(), P(), P()),
        out_specs=(over_i, over_i, over_j, over_i, part, part, part, part),
        check_vma=False,
    )
```

```python
import jax
import jax.numpy as jnp
from jax import lax
from jax.experimental import pallas as pl
from jax.experimental.pallas import tpu as pltpu
from jax.sharding import PartitionSpec as P

epsilon = 1e-05
F32 = jnp.float32
BF16 = jnp.bfloat16
MESH = pl.DeviceIdType.MESH
N = 128


def partner(p):
    return {"rows": p // 16, "blk": lax.rem(p, 16)}


def rows_norm(x):
    centred = x - jnp.mean(x, axis=-1, keepdims=True)
    inverse = lax.rsqrt(jnp.mean(centred * centred, axis=-1, keepdims=True) + epsilon)
    return centred * inverse, inverse


def rows_back(normed, inverse, up):
    first = jnp.mean(up, axis=-1, keepdims=True)
    second = jnp.mean(up * normed, axis=-1, keepdims=True)
    return inverse * (up - first - normed * second)


def dot(a, b, ca, cb):
    return lax.dot_general(a, b, (((ca,), (cb,)), ((), ())), preferred_element_type=F32)


def swap2(a, b):
    low = lax.broadcasted_iota(jnp.int32, a.shape, 1) < 64
    return (
        jnp.where(low, a, pltpu.roll(b, 64, 1)),
        jnp.where(low, pltpu.roll(a, 64, 1), b),
    )


def swap4(xs):
    y0, y2 = swap2(xs[0], xs[2])
    y1, y3 = swap2(xs[1], xs[3])
    low = (lax.broadcasted_iota(jnp.int32, y0.shape, 1) & 32) == 0
    outs = []
    for a, b in ((y0, y1), (y2, y3)):
        outs.append(jnp.where(low, a, pltpu.roll(b, 32, 1)))
        outs.append(jnp.where(low, pltpu.roll(a, 96, 1), b))
    return outs


def rows_at(start, size, step):
    return pl.ds(pl.multiple_of(start, step), size)


def kernel(
    left_hbm, right_hbm, mid_hbm, cot_hbm, lw_hbm, rw_hbm, gw_hbm, ow_hbm,
    update_hbm, gleft_hbm, gright_hbm, gmid_hbm, dleft_hbm, dright_hbm, dgate_hbm, dout_hbm,
    update_ref, gleft_ref, gright_ref, gmid_ref, dleft_ref, dright_ref, dgate_ref, dout_ref,
    left_ref, right_ref, mid_ref, cot_ref, lw_ref, rw_ref, gw_ref, ow_ref,
    wide, send_a, send_b, send_c, send_d, recv_a, recv_b, recv_c, recv_d,
    norm_l, norm_r, inv_l, inv_r, in_l, in_r, lin, sw,
    lwt, rwt, mid_norm, mid_inv, mid_t, gate, head_back, tri_in,
    lt, rt, tri, tb, lb, rb,
    grads_l, grads_r, sums, late_sums, early_send, early_held, late_held,
    early_part, late_part, early_parts, late_parts, early_all, late_all, sems, arrive_sems, fetch_sems, store_sems,
):
    my_row, my_blk = lax.axis_index("rows"), lax.axis_index("blk")
    me = my_row * 16 + my_blk
    barrier = pltpu.get_barrier_semaphore()
    fetches = [
        pltpu.make_async_copy(src, dst, fetch_sems.at[n]) for n, (src, dst) in enumerate((
            (left_hbm, left_ref), (right_hbm, right_ref), (lw_hbm, lw_ref), (rw_hbm, rw_ref),
            (mid_hbm, mid_ref), (gw_hbm, gw_ref), (cot_hbm, cot_ref), (ow_hbm, ow_ref)))]
    for fetch in fetches:
        fetch.start()
    stores = []

    def store(*pairs):
        for src, dst in pairs:
            stores.append(pltpu.make_async_copy(src, dst, store_sems.at[len(stores)]))
            stores[-1].start()

    def copy(src, dst, k, p, arrive=None):
        return pltpu.make_async_remote_copy(
            src_ref=src, dst_ref=dst, send_sem=sems.at[2 * k],
            recv_sem=sems.at[2 * k + 1] if arrive is None else arrive,
            device_id=partner(p), device_id_type=MESH)

    def greet(o, c):
        pl.semaphore_signal(
            barrier, inc=1, device_id=partner(lax.rem(me + o, N)), device_id_type=MESH)
        return c

    lax.fori_loop(1, N, greet, 0)

    def pair(g):
        return lax.rem(me // 32 + g, 4), lax.rem(me // 32 + 4 - g, 4)

    def spread(send, recv, k, fill=True):
        if fill:
            recv[me] = wide[rows_at(me * 16, 16, 16), :].astype(BF16)
        else:
            recv[me] = send[me]
        for g in range(4):
            def step(o, c):
                p = pair(g)[0] * 32 + lax.rem(me + o, 32)
                if fill:
                    send[p] = wide[rows_at(p * 16, 16, 16), :].astype(BF16)
                copy(send.at[p], recv.at[me], k, p, arrive_sems.at[4 * k + g]).start()
                return c
            lax.fori_loop(0 if g else 1, 32, step, 0)

    def arrived(recv, k, g):
        part = pl.ds(0, 32 if g else 31)
        copy(recv.at[part], recv.at[part], k, lax.rem(me + 1, N), arrive_sems.at[4 * k + g]).wait_recv()
        return pair(g)[1]

    def widen_part(recv, h):
        def step(t, c):
            at = h * 32 + t * 16
            wide[rows_at(at * 16, 256, 256), :] = (
                recv[rows_at(at, 16, 16)].astype(F32).reshape(256, 128))
            return c
        lax.fori_loop(0, 2, step, 0)

    def widen(recv, k):
        for g in range(4):
            widen_part(recv, arrived(recv, k, g))

    for fetch in fetches[:4]:
        fetch.wait()
    lwt[...] = lw_ref[...].astype(F32).T.astype(BF16)
    rwt[...] = rw_ref[...].astype(F32).T.astype(BF16)

    def norm_step(t, c):
        at = rows_at(t * 128, 128, 128)
        for ref, normed, inverse in ((left_ref, norm_l, inv_l), (right_ref, norm_r, inv_r)):
            n, i = rows_norm(ref[at, :].astype(F32))
            normed[at, :] = n
            inverse[at, :] = jnp.broadcast_to(i, n.shape)
        return c

    lax.fori_loop(0, 8, norm_step, 0)

    def chunk(ref, q, side):
        if side == 0:
            return jnp.concatenate([ref[pl.ds(q + 8 * h, 64, stride=16), :] for h in range(2)], axis=0)
        return jnp.concatenate([ref[pl.ds(q + 8 * h, 32, stride=32), :] for h in range(4)], axis=0)

    def project(q, c):
        for side, (normed, inputs, wt) in enumerate(((norm_l, in_l, lwt), (norm_r, in_r, rwt))):
            x = chunk(normed, q, side).astype(BF16)
            inputs[q] = x
            pre = dot(wt[...], x, 1, 1)
            linear, switch = pre[:N], jax.nn.sigmoid(pre[N:])
            lin[side * 8 + q] = linear
            sw[side * 8 + q] = switch
            wide[pl.ds(side * 8 + q, N, stride=16), :] = linear * switch
        return c

    lax.fori_loop(0, 8, project, 0)

    pl.semaphore_wait(barrier, N - 1)
    spread(send_a, recv_a, 0)

    for g in range(4):
        h = arrived(recv_a, 0, g)
        at = rows_at(h * 128, 128, 128)

        def unpack_left(n, c):
            tiles = [[recv_a[h * 32 + 16 * v + n * 4 + u].astype(F32)[:8] for v in range(2)] for u in range(4)]
            outs = [out for e, o in tiles for out in swap2(e, o)]
            lt[rows_at(n * 64, 64, 64), at] = jnp.concatenate(outs, axis=0).astype(BF16)
            return c

        def unpack_right(n, c):
            r = h * 2 + n
            tiles = [recv_a[r * 16 + t].astype(F32)[8:] for t in range(16)]
            outs = [jnp.concatenate(swap4(tiles[4 * v:4 * v + 4]), axis=0) for v in range(4)]
            rt[rows_at(r * 32, 32, 32), :] = jnp.concatenate(outs, axis=1).astype(BF16)
            return c

        lax.fori_loop(0, 4, unpack_left, 0)
        lax.fori_loop(0, 2, unpack_right, 0)

    for h in range(4):
        tri[h * 128:(h + 1) * 128, :] = dot(lt[:, h * 128:(h + 1) * 128], rt[...], 0, 0)

    def pack_tri(r, c):
        rows = tri[rows_at(r * 64, 64, 64), :]
        outs = [swap4([rows[16 * v:16 * v + 16, g * 128:(g + 1) * 128] for v in range(4)]) for g in range(4)]
        for g in range(4):
            for t in range(4):
                send_b[r * 16 + 4 * g + t] = outs[g][t].astype(BF16)
        return c

    lax.fori_loop(0, 8, pack_tri, 0)

    spread(send_b, recv_b, 1, fill=False)

    def middle(q, c):
        slots = (2 * q, 2 * q + 1)
        xs = [mid_ref[:, s].astype(F32).reshape(N, 128) for s in slots]
        norms = [rows_norm(x) for x in xs]
        gates = [jax.nn.sigmoid(dot(n.astype(BF16), gw_ref[...], 1, 0)) for n, _ in norms]
        turned = [n.T.astype(BF16) for n, _ in norms]
        for s, (n, i), g, t in zip(slots, norms, gates, turned):
            mid_norm[s] = n
            mid_inv[s] = jnp.broadcast_to(i, n.shape)
            mid_t[s] = t
            gate[s] = g
        return c

    for fetch in fetches[4:]:
        fetch.wait()
    lax.fori_loop(0, 8, middle, 0)

    widen(recv_b, 1)

    def heads(q, c):
        slots = (2 * q, 2 * q + 1)
        at = [pl.ds(s, N, stride=16) for s in slots]
        xs = [wide[a, :] for a in at]
        backs = [(cot_ref[:, s].astype(F32).reshape(N, 128) * gate[s]).astype(BF16) for s in slots]
        ups = [dot(ow_ref[...], back, 1, 1) for back in backs]
        outs = []
        for x, up in zip(xs, ups):
            centred = x - jnp.mean(x, axis=0, keepdims=True)
            inverse = lax.rsqrt(jnp.mean(centred * centred, axis=0, keepdims=True) + epsilon)
            normed = centred * inverse
            first = jnp.mean(up, axis=0, keepdims=True)
            second = jnp.mean(up * normed, axis=0, keepdims=True)
            outs.append((normed, inverse * (up - first - normed * second)))
        for s, a, back, (normed, out) in zip(slots, at, backs, outs):
            head_back[s] = back
            tri_in[s] = normed.astype(BF16)
            wide[a, :] = out
        return c

    lax.fori_loop(0, 8, heads, 0)
    spread(send_c, recv_c, 2)

    sums[...] = jnp.zeros_like(sums)

    def rest(q, c):
        slots = (2 * q, 2 * q + 1)
        gates = [gate[s] for s in slots]
        hs = [dot(tri_in[s].astype(F32).T.astype(BF16), ow_ref[...], 1, 0) for s in slots]
        backs = [
            (cot_ref[:, s].astype(F32).reshape(N, 128) * h * g * (1.0 - g)).astype(BF16)
            for s, h, g in zip(slots, hs, gates)]
        outs = [
            rows_back(mid_norm[s], mid_inv[s], dot(b, gw_ref[...], 1, 1)).astype(BF16)
            for s, b in zip(slots, backs)]
        gate_sum = [dot(mid_t[s], b, 1, 0) for s, b in zip(slots, backs)]
        out_sum = [dot(tri_in[s], head_back[s], 1, 0) for s in slots]
        sums[0:128, :] += gate_sum[0] + gate_sum[1]
        sums[128:256, :] += out_sum[0] + out_sum[1]
        for s, g, h, out in zip(slots, gates, hs, outs):
            update_ref[:, s] = (g * h).astype(BF16).reshape(4, 32, 128)
            gmid_ref[:, s] = out.reshape(4, 32, 128)
        return c

    lax.fori_loop(0, 3, rest, 0)

    def over_blk(o):
        return my_row * 16 + lax.rem(my_blk + o, 16)

    def sum_scatter(src, send, held, k):
        send[...] = src[...].astype(BF16)
        rows = held.shape[1]
        for o in range(1, 16):
            p = over_blk(o)
            at = rows_at(lax.rem(p, 16) * rows, rows, rows)
            copy(send.at[at], held.at[my_blk], k, p).start()
        held[my_blk] = send[rows_at(my_blk * rows, rows, rows), :]

    def sum_exchange(held, part, parts, k):
        slots = held.shape[0] // 16
        most = held.at[pl.ds(0, 15 * slots)]
        copy(most, most, k, over_blk(1)).wait_recv()
        part[...] = jnp.concatenate(
            [jnp.sum(held[16 * n:16 * n + 16].astype(F32), axis=0) for n in range(slots)], axis=0)
        for o in range(1, 8):
            copy(part, parts.at[my_row], k + 1, lax.rem(me + 16 * o, N)).start()
        parts[my_row] = part[...]

    def sum_spread(parts, whole, k):
        copy(parts.at[pl.ds(0, 7)], parts.at[pl.ds(0, 7)], k + 1, lax.rem(me + 16, N)).wait_recv()
        rows = parts.shape[1]
        at = rows_at(my_blk * rows, rows, rows)
        whole[at, :] = jnp.sum(parts[...], axis=0).astype(BF16)
        for o in range(1, 16):
            copy(whole.at[at], whole.at[at], k + 2, over_blk(o)).start()

    def sum_wait(whole, k):
        most = pl.ds(0, whole.shape[0] // 16 * 15)
        copy(whole.at[most], whole.at[most], k + 2, over_blk(1)).wait_recv()

    def sum_sent(held, whole, parts, k):
        most = held.at[pl.ds(0, held.shape[0] // 16 * 15)]
        copy(most, most, k, over_blk(1)).wait_send()
        most = pl.ds(0, whole.shape[0] // 16 * 15)
        copy(parts.at[pl.ds(0, 7)], parts.at[pl.ds(0, 7)], k + 1, over_blk(1)).wait_send()
        copy(whole.at[most], whole.at[most], k + 2, over_blk(1)).wait_send()

    for g in range(4):
        h = arrived(recv_c, 2, g)
        at = rows_at(h * 128, 128, 128)

        def unpack_tb(n, c):
            r = h * 2 + n
            tiles = [recv_c[r * 16 + t].astype(F32) for t in range(16)]
            outs = [jnp.concatenate(swap4(tiles[4 * v:4 * v + 4]), axis=0) for v in range(4)]
            tb[rows_at(r * 64, 64, 64), :] = jnp.concatenate(outs, axis=1).astype(BF16)
            return c

        lax.fori_loop(0, 2, unpack_tb, 0)
        lb[...] = dot(rt[...], tb[at, :], 1, 1)
        if g == 0:
            rb[...] = dot(lt[:, at], tb[at, :], 1, 0)
        else:
            rb[...] += dot(lt[:, at], tb[at, :], 1, 0)

        def pack_left(n, c):
            tiles = [lb[rows_at((n * 4 + u) * 16, 16, 16), :] for u in range(4)]
            outs = [swap2(tile[:8], tile[8:]) for tile in tiles]
            for u in range(4):
                for v in range(2):
                    wide[rows_at((h * 32 + 16 * v + n * 4 + u) * 16, 8, 8), :] = outs[u][v]
            return c

        lax.fori_loop(0, 4, pack_left, 0)

    def pack_right(r, c):
        rows = rb[rows_at(r * 32, 32, 32), :]
        outs = [swap4([rows[8 * v:8 * v + 8, g * 128:(g + 1) * 128] for v in range(4)]) for g in range(4)]
        for g in range(4):
            for t in range(4):
                wide[rows_at((r * 16 + 4 * g + t) * 16 + 8, 8, 8), :] = outs[g][t]
        return c

    lax.fori_loop(0, 8, pack_right, 0)
    spread(send_d, recv_d, 3)

    lax.fori_loop(3, 8, rest, 0)
    store((update_ref, update_hbm), (gmid_ref, gmid_hbm))

    sum_scatter(sums, early_send, early_held, 4)


    sides = ((norm_l, inv_l, in_l, lw_ref, grads_l), (norm_r, inv_r, in_r, rw_ref, grads_r))
    for g in range(4):
        h = arrived(recv_d, 3, g)
        widen_part(recv_d, h)
        low = rows_at(h * 32, 32, 32)
        high = rows_at(h * 32 + 128, 32, 32)
        for side, (_, _, inputs, _, grads) in enumerate(sides):
            ups, switches = [], []
            for q in range(8):
                up = wide[pl.ds(h * 512 + side * 8 + q, 32, stride=16), :]
                linear, switch = lin[side * 8 + q, low, :], sw[side * 8 + q, low, :]
                ups.append((up * switch).astype(BF16))
                switches.append((up * linear * switch * (1.0 - switch)).astype(BF16))
                grads[q, low, :] = ups[q]
                grads[q, high, :] = switches[q]
            joined = jnp.concatenate(
                [jnp.concatenate(ups, axis=1), jnp.concatenate(switches, axis=1)], axis=0)
            late_sums[rows_at(h * 128 + side * 64, 64, 64), :] = dot(
                joined, inputs[...].reshape(1024, 128), 1, 0)
        for o in range(1, 16):
            p = over_blk(o)
            piece = rows_at(h * 128 + lax.rem(p, 16) * 8, 8, 8)
            copy(late_sums.at[piece], late_held.at[h * 16 + my_blk], 7, p).start()
        late_held[h * 16 + my_blk] = late_sums[rows_at(h * 128 + my_blk * 8, 8, 8), :]
    sum_exchange(early_held, early_part, early_parts, 4)

    def back_step(q, c):
        outs = [
            rows_back(
                chunk(normed, q, side), chunk(inverse, q, side), dot(w_ref[...], grads[q], 1, 0).T)
            for side, (normed, inverse, _, w_ref, grads) in enumerate(sides)]
        for h in range(2):
            norm_l[pl.ds(q + 8 * h, 64, stride=16), :] = outs[0][h * 64:(h + 1) * 64]
        for h in range(4):
            norm_r[pl.ds(q + 8 * h, 32, stride=32), :] = outs[1][h * 32:(h + 1) * 32]
        return c

    lax.fori_loop(0, 8, back_step, 0)

    def round_step(t, c):
        at = rows_at(t * 128, 128, 128)
        gleft_ref[at, :] = norm_l[at, :].astype(BF16)
        gright_ref[at, :] = norm_r[at, :].astype(BF16)
        return c

    lax.fori_loop(0, 8, round_step, 0)
    store((gleft_ref, gleft_hbm), (gright_ref, gright_hbm))
    sum_exchange(late_held, late_part, late_parts, 7)
    sum_spread(early_parts, early_all, 4)
    sum_spread(late_parts, late_all, 7)
    sum_wait(early_all, 4)
    dgate_ref[...] = early_all[0:128, :].astype(F32)
    dout_ref[...] = early_all[128:256, :].astype(F32)
    sum_wait(late_all, 7)
    whole = late_all[...].astype(F32)
    for side, target in enumerate((dleft_ref, dright_ref)):
        target[...] = jnp.concatenate([
            whole[b * 32 + h * 8:b * 32 + h * 8 + 8]
            for kind in range(2) for h in range(4)
            for b in range(side * 8 + kind * 4, side * 8 + kind * 4 + 4)], axis=0).T
    store((dgate_ref, dgate_hbm), (dout_ref, dout_hbm), (dleft_ref, dleft_hbm), (dright_ref, dright_hbm))

    for k, send in enumerate((send_a, send_b, send_c, send_d)):
        most = send.at[pl.ds(0, N - 1)]
        copy(most, most, k, lax.rem(me + 1, N)).wait_send()
    sum_sent(early_held, early_all, early_parts, 4)
    sum_sent(late_held, late_all, late_parts, 7)
    for one in stores:
        one.wait()


def store_kernel(*refs):
    sources, targets, held, sems = refs[:8], refs[8:16], refs[16:24], refs[24]
    reads = [pltpu.make_async_copy(s, h, sems.at[n]) for n, (s, h) in enumerate(zip(sources, held))]
    writes = [pltpu.make_async_copy(h, t, sems.at[8 + n]) for n, (h, t) in enumerate(zip(held, targets))]
    for read in reads:
        read.start()
    for read, write in zip(reads, writes):
        read.wait()
        write.start()
    for write in writes:
        write.wait()


def per_device(left, right, middle, cotangent, lw, rw, gw, ow):
    tile = (N, 16, 128)
    pairs, flat, mids = (1024, 128), ((1024, 128), BF16), ((4, 16, 32, 128), BF16)
    results = [mids, flat, flat, mids] + [((128, 256), F32)] * 2 + [((128, 128), F32)] * 2
    shapes = [jax.ShapeDtypeStruct(s, t) for s, t in results]
    scratch = (
        results + [flat, flat, mids, mids] + [((128, 256), BF16)] * 2 + [((128, 128), BF16)] * 2
        + [((2048, 128), F32)] + [(tile, BF16)] * 8
        + [(pairs, F32)] * 4 + [((8, 128, 128), BF16)] * 2 + [((16, 128, 128), F32)] * 2
        + [((256, 128), BF16)] * 2 + [((16, 128, 128), F32)] * 2 + [((16, 128, 128), BF16)]
        + [((16, 128, 128), F32)] + [((16, 128, 128), BF16)] * 2
        + [((256, 512), BF16)] * 2 + [((512, 512), F32), ((512, 512), BF16)] + [((256, 128), F32), ((256, 512), F32)]
        + [((8, 256, 128), BF16)] * 2
        + [((256, 128), F32), ((512, 128), F32), ((256, 128), BF16)]
        + [((16, 16, 128), BF16), ((64, 8, 128), F32), ((16, 128), F32), ((32, 128), F32)]
        + [((8, 16, 128), F32), ((8, 32, 128), F32), ((256, 128), BF16), ((512, 128), BF16)]
    )
    outs = pl.pallas_call(
        kernel,
        out_shape=shapes,
        in_specs=[pl.BlockSpec(memory_space=pltpu.HBM)] * 8,
        out_specs=[pl.BlockSpec(memory_space=pltpu.HBM)] * 8,
        scratch_shapes=[pltpu.VMEM(s, t) for s, t in scratch] + [
            pltpu.SemaphoreType.DMA((20,)), pltpu.SemaphoreType.DMA((16,)), pltpu.SemaphoreType.DMA((8,)), pltpu.SemaphoreType.DMA((8,))],
        compiler_params=pltpu.CompilerParams(
            collective_id=0, has_side_effects=True, vmem_limit_bytes=61 * 2**20),
    )(
        left.reshape(pairs), right.reshape(pairs),
        middle.reshape(mids[0]), cotangent.reshape(mids[0]), lw, rw, gw, ow,
    )
    outs = pl.pallas_call(
        store_kernel,
        out_shape=shapes,
        in_specs=[pl.BlockSpec(memory_space=pltpu.HBM)] * 8,
        out_specs=[pl.BlockSpec(memory_space=pltpu.HBM)] * 8,
        scratch_shapes=[pltpu.VMEM(s, t) for s, t in results] + [pltpu.SemaphoreType.DMA((16,))],
        compiler_params=pltpu.CompilerParams(vmem_limit_bytes=61 * 2**20),
    )(*outs)
    return (
        outs[0].reshape(64, 32, 128), outs[1].reshape(64, 16, 128),
        outs[2].reshape(32, 32, 128), outs[3].reshape(64, 32, 128), *outs[4:],
    )


def solution(mesh):
    over_i = P(("rep", "rows"), "blk", None)
    over_j = P(("rep", "blk"), "rows", None)
    part = P("rep", None)
    return jax.shard_map(
        per_device,
        mesh=mesh,
        in_specs=(over_i, over_j, over_i, over_i, P(), P(), P(), P()),
        out_specs=(over_i, over_i, over_j, over_i, part, part, part, part),
        check_vma=False,
    )
```
